32 devices in a mesh: wide: 8 (over z, y), narrow: 4 (over x, core).
Axes of the slice: x: 2, y: 2, z: 4, core: 2. Of those that a mesh axis runs over, the one named last changes fastest.
Arguments:
- dense: bfloat16 [4096, 256], P(('wide', 'narrow')), may hold values from -6 to 6
- pooled: bfloat16 [4096, 8, 256], P(('wide', 'narrow')), may hold values from -1.5 to 1.5
- w_top: bfloat16 [1024, 292], replicated, may hold values from -0.375 to 0.375
- bias: float32 [1024], replicated, may hold values from -3 to 3
- d_hidden: bfloat16 [4096, 1024], P(('wide', 'narrow')), may hold values from -6 to 6
- bag_ids: int32 [8, 4096, 2], P('wide'), may hold values from 0 to 4095
- tables: float32 [8, 4096, 256], P('wide', 'narrow'), may hold values from -6 to 6
- accum: float32 [8, 4096], P('wide', 'narrow'), may hold values from 0.1 to 10
Outputs:
- new_tables: float32 [8, 4096, 256], P('wide', 'narrow')
- new_accum: float32 [8, 4096], P('wide', 'narrow')
- w_grad: float32 [1024, 292], P('wide')
The draws below stay inside these ranges and needn't reach their ends.
All inputs are finite; a program needn't handle non-finite values.
Results may differ from the reference program's by a relative error of at most 0.0047.
Values may be sent and summed in bfloat16 or wider, within the bound.
No kernel may reach another device: no remote copies, remote signals or barrier semaphores. Data moves between devices by JAX's collectives and lax.ppermute only.
A program may use at most 128 MiB of HBM per device.

```python
import math
import jax
import jax.numpy as jnp
import numpy as np
from jax import lax

D = 256
H = 1024
BAG = 2
B_DEV = 128
TABLES = 8
ROWS = 4096
BATCH = 4096
I = 292


def place_ends(array, rng, low, largest):
    place = [jax.random.randint(jax.random.fold_in(rng, axis), (), 0, length) for axis, length in enumerate(array.shape)]
    main_axis = array.shape.index(max(array.shape))
    next_to = place[:main_axis] + [(place[main_axis] + 1) % array.shape[main_axis]] + place[main_axis + 1:]
    return array.at[tuple(place)].set(low).at[tuple(next_to)].set(largest)


def with_spikes(entries, rng, source, target, parts, factor):
    owner, partner = [(jnp.arange(entries.shape[dim]) // (entries.shape[dim] // parts)).reshape([-1 if axis == dim else 1 for axis in range(entries.ndim)]) for dim in (source, target)]
    chosen = jax.random.permutation(rng, parts)[partner]
    strong = (owner == chosen) | (owner == (partner + parts // 2) % parts)
    return jnp.where(strong, factor * entries, entries)


def levels(own_key, shape, shards, smallest, top_value):
    loudness = 1.0
    for dim, blocks in shards:
        heights = jax.random.uniform(jax.random.fold_in(jax.random.fold_in(own_key, 6), dim), (blocks,), jnp.float32, smallest / len(shards), top_value / len(shards))
        loudness = loudness * jnp.repeat(jnp.exp(heights), shape[dim] // blocks).reshape((-1,) + (1,) * (len(shape) - 1 - dim))
    return loudness


def rank_table(number_of, lean):
    loads = [(1 << 20) // math.isqrt(standing ** lean) + 1 for standing in range(1, number_of + 1)]
    scale = 1 + sum(loads) // (1 << 30)
    return np.cumsum(np.array([max(1, weight // scale) for weight in loads]))


def ranked(key, dims, number_of, skew):
    grid = rank_table(number_of, skew)
    ticket = jax.random.randint(jax.random.fold_in(key, 1), dims, 0, int(grid[number_of - 1]))
    rank = jnp.searchsorted(jnp.asarray(grid, jnp.int32), ticket, side="right")
    return jax.random.permutation(jax.random.fold_in(key, 2), number_of)[rank].astype(jnp.int32)


def normal_values(key, dims, scale, most, cuts=(), kind=jnp.bfloat16):
    level = levels(key, dims, cuts, -0.22, 0.18) if cuts else 1.0
    drawn = jax.random.normal(key, dims, jnp.float32) * scale * level
    return jnp.minimum(jnp.maximum(drawn, -most), most).astype(kind)


def noise_with(rng, dims, spread, reach, cuts, heavy, dtype=jnp.bfloat16):
    array = spread * jax.random.normal(rng, dims, jnp.float32)
    if cuts:
        array = array * levels(rng, dims, cuts, -0.22, 0.18)
    return jnp.clip(with_spikes(array, jax.random.fold_in(rng, 3), *heavy), -reach, reach).astype(dtype)


def setup_inputs(seed: int = 0) -> dict:
    key_list = jax.random.split(jax.random.key(seed), 9)
    return {
        "dense": normal_values(key_list[0], (BATCH, D), 1.0, 6.0, ((0, 32),)),
        "pooled": normal_values(key_list[1], (BATCH, TABLES, D), 0.25, 1.5, ((0, 32),)),
        "w_top": normal_values(key_list[2], (H, I), I ** -0.5, 0.375),
        "bias": normal_values(key_list[3], (H,), 0.5, 3.0, (), jnp.float32),
        "d_hidden": noise_with(key_list[4], (BATCH, H), 1.0, 6.0, ((0, 32),), (0, 1, 32, 2.75)),
        "bag_ids": place_ends(ranked(key_list[5], (TABLES, BATCH, BAG), ROWS, 1), jax.random.fold_in(key_list[5], 3), 0, ROWS - 1).astype(jnp.int32),
        "tables": normal_values(key_list[6], (TABLES, ROWS, D), 1.0, 6.0, ((0, 8), (1, 4)), jnp.float32),
        "accum": jnp.clip(jnp.exp(math.log(10.0) - 4.6051702 * jax.random.uniform(key_list[7], (TABLES, ROWS), jnp.float32) ** levels(key_list[7], (TABLES, ROWS), ((0, 8), (1, 4)), -0.2, 0.2)), 0.1, 10.0),
    }


def block_pass(dense_block, pooled_block, hidden_block, w_top, bias):
    feats = jnp.concatenate([dense_block[:, None, :], pooled_block], axis=1)
    wide_feats = feats.astype(jnp.float32)
    count = feats.shape[1]
    width = dense_block.shape[1]
    low_i, low_j = np.tril_indices(count, -1)
    zmat = jnp.einsum('bfd,bgd->bfg', wide_feats, wide_feats)
    z_in = jnp.concatenate([dense_block.astype(jnp.float32), zmat[:, low_i, low_j]], axis=1).astype(jnp.bfloat16)
    pre = jnp.dot(z_in, w_top.T, preferred_element_type=jnp.float32) + bias
    sig = jax.nn.sigmoid(pre)
    slope = sig * (1.0 + pre * (1.0 - sig))
    dpre = (hidden_block.astype(jnp.float32) * slope).astype(jnp.bfloat16)
    dz_full = jnp.dot(dpre, w_top, preferred_element_type=jnp.float32)
    dpairs = dz_full[:, width:]
    rows_here = dense_block.shape[0]
    dmat = jnp.zeros((rows_here, count * count), jnp.float32).at[:, low_i * count + low_j].set(dpairs)
    dmat = dmat.reshape(rows_here, count, count)
    dsym = (dmat + jnp.transpose(dmat, (0, 2, 1))).astype(jnp.bfloat16)
    dfeat = jnp.einsum('bfg,bgd->bfd', dsym.astype(jnp.float32), wide_feats)
    dpooled = dfeat[:, 1:, :].astype(jnp.bfloat16)
    term = jnp.dot(dpre.T, z_in, preferred_element_type=jnp.float32)
    return (dpooled, term)

def reference(dense, pooled, w_top, bias, d_hidden, bag_ids, tables, accum):
    blocks = BATCH // B_DEV
    dense_b = dense.reshape(blocks, B_DEV, D)
    pooled_b = pooled.reshape(blocks, B_DEV, TABLES, D)
    hidden_b = d_hidden.reshape(blocks, B_DEV, H)

    def step(carry, pieces):
        dpooled, term = block_pass(pieces[0], pieces[1], pieces[2], w_top, bias)
        return (carry + term, dpooled)
    total, dpooled_b = lax.scan(step, jnp.zeros((H, I), jnp.float32), (dense_b, pooled_b, hidden_b))
    w_grad = total / math.sqrt(BATCH)
    dpooled = dpooled_b.reshape(BATCH, TABLES, D)
    per_table = jnp.transpose(dpooled, (1, 0, 2))

    def update(pieces):
        grads, ids, table, acc = pieces
        wide_grads = grads.astype(jnp.float32)
        row_grad = jnp.zeros((ROWS, D), jnp.float32)
        for slot in range(BAG):
            row_grad = row_grad + jax.ops.segment_sum(wide_grads, ids[:, slot], num_segments=ROWS)
        acc_new = acc + lax.optimization_barrier(jnp.mean(row_grad * row_grad, axis=1))
        table_new = table - 0.1 * row_grad / (jnp.sqrt(acc_new)[:, None] + 1e-08)
        return (table_new, acc_new)
    new_tables, new_accum = lax.map(update, (per_table, bag_ids, tables, accum))
    return (new_tables, new_accum, w_grad)
```

```python
import functools
import math

import jax
import jax.numpy as jnp
import numpy as np
from jax import lax
from jax.experimental import pallas as pl
from jax.experimental.pallas import tpu as pltpu
from jax.sharding import PartitionSpec as P

NT = (((1,), (1,)), ((), ()))


def eye(n):
    r = lax.broadcasted_iota(jnp.int32, (n, n), 0)
    c = lax.broadcasted_iota(jnp.int32, (n, n), 1)
    return jnp.where(r == c, 1.0, 0.0).astype(jnp.bfloat16)


def local_kernel(
    place, dense_in, pooled_in, w_in, bias_in, d_hidden_in,
    out, keep, send,
    dense, pooled, w_t, bias, d_hidden,
    pooled32, feat_t, zrows, z_t, dp_t, wg, sems,
):
    moves = [
        pltpu.make_async_copy(source, target, sems.at[i])
        for i, (source, target) in enumerate(
            ((pooled_in, pooled), (dense_in, dense), (w_in, w_t), (bias_in, bias), (d_hidden_in, d_hidden))
        )
    ]
    for move in moves:
        move.start()
    samples, width = dense.shape
    tables = pooled.shape[0] // samples
    count = tables + 1
    low_i, low_j = np.tril_indices(count, -1)
    pairs = len(low_i)
    of_pair = {}
    for p, (i, j) in enumerate(zip(low_i, low_j)):
        of_pair[int(i), int(j)] = of_pair[int(j), int(i)] = p
    wide, core = place[0], place[1]

    moves[0].wait()
    for h in range(width // 128):
        pooled32[h] = pooled[:, h * 128 : (h + 1) * 128].astype(jnp.float32)
    ident = eye(width)
    moves[1].wait()
    feat_t[0] = lax.dot_general(ident, dense[...], NT, preferred_element_type=jnp.float32)
    for t in range(tables):
        rows = jnp.concatenate(
            [pooled32[h, pl.ds(t, samples, stride=tables), :] for h in range(width // 128)], axis=1
        ).astype(jnp.bfloat16)
        feat_t[t + 1] = lax.dot_general(ident, rows, NT, preferred_element_type=jnp.float32)

    def products(c, sums):
        f = [feat_t[i, pl.ds(pl.multiple_of(c * 8, 8), 8), :] for i in range(count)]
        return tuple(s + f[i] * f[j] for s, i, j in zip(sums, low_i, low_j))

    zero = jnp.zeros((8, samples), jnp.float32)
    sums = lax.fori_loop(0, width // 8, products, (zero,) * pairs, unroll=4)
    zrows[...] = jnp.zeros_like(zrows)
    for p in range(pairs):
        zrows[p : p + 1, :] = jnp.sum(sums[p], axis=0, keepdims=True)

    z_t[:width, :] = feat_t[0].astype(jnp.bfloat16)
    extra = z_t.shape[0] - width
    z_t[width:, :] = zrows[:extra, :].astype(jnp.bfloat16)
    z_pairs = zrows[...].T[:, :pairs].astype(jnp.bfloat16)
    for move in moves[2:]:
        move.wait()
    w_pairs = w_t[width : width + pairs, :]
    pre = (
        jnp.dot(dense[...], w_t[:width, :], preferred_element_type=jnp.float32)
        + jnp.dot(z_pairs, w_pairs, preferred_element_type=jnp.float32)
        + bias[...]
    )
    sig = 1.0 / (1.0 + jnp.exp(-pre))
    slope = sig * (1.0 + pre * (1.0 - sig))
    dpre = (d_hidden[...].astype(jnp.float32) * slope).astype(jnp.bfloat16)
    dsym = lax.dot_general(w_pairs, dpre, NT, preferred_element_type=jnp.float32)
    dsym = dsym.astype(jnp.bfloat16).astype(jnp.float32)

    spread = [jnp.broadcast_to(dsym[p : p + 1, :], (8, samples)) for p in range(pairs)]

    def gradients(c, carry):
        for h in range(2):
            at = pl.ds(pl.multiple_of(c * 16 + h * 8, 8), 8)
            f = [feat_t[i, at, :] for i in range(count)]
            for t in range(tables):
                total = None
                for g in range(count):
                    if g != t + 1:
                        term = spread[of_pair[t + 1, g]] * f[g]
                        total = term if total is None else total + term
                dp_t[t, at, :] = total
        return carry

    lax.fori_loop(0, width // 16, gradients, 0)
    ident_s = eye(samples)
    for t in range(tables):
        got = lax.dot_general(ident_s, dp_t[t].astype(jnp.bfloat16), NT, preferred_element_type=jnp.float32)
        out[jnp.bitwise_xor(wide, t)] = got.astype(jnp.bfloat16)

    half = wg.shape[1]
    for h in range(2):
        wg[h] = jnp.dot(z_t[h * half : (h + 1) * half, :], dpre, preferred_element_type=jnp.float32)
    keep[...] = wg[core]
    send[...] = wg[1 - core].astype(send.dtype)


def local_part(place, dense, pooled, w_t, bias, d_hidden, send_type):
    samples, width = dense.shape
    tables = pooled.shape[1]
    hidden = w_t.shape[1]
    padded = -(-w_t.shape[0] // 64) * 64
    half = padded // 2
    vmem = pl.BlockSpec(memory_space=pltpu.VMEM)
    return pl.pallas_call(
        local_kernel,
        out_shape=(
            jax.ShapeDtypeStruct((tables, samples, width), jnp.bfloat16),
            jax.ShapeDtypeStruct((half, hidden), jnp.float32),
            jax.ShapeDtypeStruct((half, hidden), send_type),
        ),
        in_specs=[pl.BlockSpec(memory_space=pltpu.SMEM)] + [pl.BlockSpec(memory_space=pltpu.HBM)] * 5,
        out_specs=(vmem,) * 3,
        scratch_shapes=[
            pltpu.VMEM((samples, width), dense.dtype),
            pltpu.VMEM((samples * tables, width), pooled.dtype),
            pltpu.VMEM(w_t.shape, w_t.dtype),
            pltpu.VMEM((1, hidden), bias.dtype),
            pltpu.VMEM((samples, hidden), d_hidden.dtype),
            pltpu.VMEM((width // 128, samples * tables, 128), jnp.float32),
            pltpu.VMEM((tables + 1, width, samples), jnp.float32),
            pltpu.VMEM((128, samples), jnp.float32),
            pltpu.VMEM((padded, samples), jnp.bfloat16),
            pltpu.VMEM((tables, width, samples), jnp.float32),
            pltpu.VMEM((2, half, hidden), jnp.float32),
            pltpu.SemaphoreType.DMA((5,)),
        ],
        compiler_params=pltpu.CompilerParams(vmem_limit_bytes=60 * 2**20),
    )(place, dense, pooled.reshape(samples * tables, width), w_t, bias.reshape(1, hidden), d_hidden)


def update_kernel(place, ids, table, accum, *refs):
    grads, (new_table, new_accum, ids_a, ids_b) = refs[:4], refs[4:]
    rows, width = table.shape
    blocks, samples = grads[0].shape[:2]
    n_narrow = 4
    wide, narrow = place[0], place[2]
    step = 16
    down = lax.broadcasted_iota(jnp.int32, (step, samples), 0)
    for j in range(4):
        for k in range(blocks):
            at = jnp.bitwise_xor(wide, k) * n_narrow + jnp.bitwise_xor(narrow, j)
            local = ids[:, pl.ds(pl.multiple_of(at * samples, samples), samples)] - narrow * rows
            for s, keep in enumerate((ids_a, ids_b)):
                keep[j, :, k * samples : (k + 1) * samples] = (
                    jnp.broadcast_to(local[s : s + 1, :], (step, samples)) - down
                ).astype(jnp.int16)
    tile = 128
    one, none = jnp.bfloat16(1), jnp.bfloat16(0)
    scale_rows = width

    def tile_step(m, carry):
        base = m * tile
        total = jnp.zeros((tile, width), jnp.float32)
        for j in range(4):
            a, b = ids_a[j], ids_b[j]
            parts = []
            for i in range(tile // step):
                want = (base + i * step).astype(jnp.int16)
                parts.append(jnp.where(a == want, one, none) + jnp.where(b == want, one, none))
            hot = jnp.concatenate(parts, axis=0)
            total += jnp.dot(hot, grads[j][...].reshape(blocks * samples, width), preferred_element_type=jnp.float32)
        at = pl.ds(pl.multiple_of(base, tile), tile)
        mean = jnp.sum(total * total, axis=1, keepdims=True) * (1.0 / width)
        row = jnp.broadcast_to(mean, (tile, tile)).T[:1, :]
        fresh = accum[:, at] + row
        new_accum[:, at] = fresh
        rate = 0.1 / (jnp.sqrt(fresh) + 1e-8)
        rate = jnp.broadcast_to(rate, (tile, tile)).T
        for h in range(width // tile):
            cols = slice(h * tile, (h + 1) * tile)
            new_table[at, cols] = table[at, cols] - total[:, cols] * rate
        return carry

    lax.fori_loop(0, rows // tile, tile_step, 0)


def update_part(place, ids, table, accum, grads):
    rows, width = table.shape
    blocks, samples = grads[0].shape[:2]
    vmem = pl.BlockSpec(memory_space=pltpu.VMEM)
    return pl.pallas_call(
        update_kernel,
        out_shape=(
            jax.ShapeDtypeStruct((rows, width), jnp.float32),
            jax.ShapeDtypeStruct((1, rows), jnp.float32),
        ),
        in_specs=[pl.BlockSpec(memory_space=pltpu.SMEM)] + [vmem] * 7,
        out_specs=(vmem,) * 2,
        scratch_shapes=[pltpu.VMEM((4, 16, blocks * samples), jnp.int16)] * 2,
        compiler_params=pltpu.CompilerParams(vmem_limit_bytes=60 * 2**20),
    )(place, ids, table, accum, *grads)


def row_sums(grads, ids, offset, count):
    local = ids - offset
    local = jnp.where((local >= 0) & (local < count), local, count)
    result = jnp.zeros((count, grads.shape[1]), jnp.float32)
    for slot in range(ids.shape[1]):
        result = result + jax.ops.segment_sum(grads, local[:, slot], num_segments=count + 1)[:count]
    return result


def plain_body(dense, pooled, w_top, bias, d_hidden, bag_ids, tables, accum):
    samples = dense.shape[0]
    width = dense.shape[1]
    n_wide = lax.axis_size("wide")
    n_narrow = lax.axis_size("narrow")
    total = samples * n_wide * n_narrow
    feats = jnp.concatenate([dense[:, None, :], pooled], axis=1)
    count = feats.shape[1]
    low_i, low_j = np.tril_indices(count, -1)
    zmat = jnp.einsum("bfd,bgd->bfg", feats, feats, preferred_element_type=jnp.float32)
    z_in = jnp.concatenate([dense.astype(jnp.float32), zmat[:, low_i, low_j]], axis=1).astype(
        jnp.bfloat16
    )
    pre = jnp.dot(z_in, w_top.T, preferred_element_type=jnp.float32) + bias
    sig = jax.nn.sigmoid(pre)
    slope = sig * (1.0 + pre * (1.0 - sig))
    dpre = (d_hidden.astype(jnp.float32) * slope).astype(jnp.bfloat16)
    dz_full = jnp.dot(dpre, w_top, preferred_element_type=jnp.float32)
    dpairs = dz_full[:, width:]
    dmat = jnp.zeros((samples, count * count), jnp.float32).at[:, low_i * count + low_j].set(dpairs)
    dmat = dmat.reshape(samples, count, count)
    dsym = (dmat + jnp.transpose(dmat, (0, 2, 1))).astype(jnp.bfloat16)
    dfeat = jnp.einsum("bfg,bgd->bfd", dsym, feats, preferred_element_type=jnp.float32)
    dpooled = dfeat[:, 1:, :].astype(jnp.bfloat16)
    part = lax.slice_in_dim(dpre, 0, w_top.shape[0] // n_wide * lax.axis_size("wide"), axis=1)
    wide_part = lax.psum_scatter(
        jnp.dot(part.T, z_in, preferred_element_type=jnp.float32),
        "wide",
        scatter_dimension=0,
        tiled=True,
    )
    w_grad = lax.psum(wide_part, "narrow") / math.sqrt(total)
    owned = lax.all_to_all(dpooled, "wide", split_axis=1, concat_axis=0, tiled=True).reshape(
        n_wide * samples, width
    )
    bag = bag_ids.shape[2]
    ids_four = bag_ids[0].reshape(n_wide, n_narrow, samples, bag)
    rows_dev = tables.shape[1]
    narrow_pos = lax.axis_index("narrow")
    every = lax.all_gather(owned, "narrow", axis=0, tiled=True)
    ids_all = jnp.transpose(ids_four, (1, 0, 2, 3)).reshape(-1, bag)
    row_grad = row_sums(every.astype(jnp.float32), ids_all, narrow_pos * rows_dev, rows_dev)
    acc_new = accum[0] + jnp.mean(row_grad * row_grad, axis=1)
    table_new = tables[0] - 0.1 * row_grad / (jnp.sqrt(acc_new)[:, None] + 1e-08)
    return (table_new[None], acc_new[None], w_grad)


def body(dense, pooled, w_top, bias, d_hidden, bag_ids, tables, accum):
    n_wide, n_narrow = lax.axis_size("wide"), lax.axis_size("narrow")
    samples, count = dense.shape[0], pooled.shape[1]
    rows, width = tables.shape[1:]
    inputs = w_top.shape[1]
    total = samples * n_wide * n_narrow
    if n_narrow != 4 or n_wide & (n_wide - 1) or count != n_wide or total * width > 2**21:
        return plain_body(dense, pooled, w_top, bias, d_hidden, bag_ids, tables, accum)
    wide, narrow = lax.axis_index("wide"), lax.axis_index("narrow")
    core, chip = narrow % 2, narrow // 2
    place = jnp.stack([wide, core, narrow]).astype(jnp.int32)

    def swap(array, axis, bit):
        n = lax.axis_size(axis)
        return lax.ppermute(array, axis, [(i, i ^ bit) for i in range(n)])

    out, keep, send = local_part(place, dense, pooled, w_top.T, bias, d_hidden, jnp.float32)
    owned = jnp.stack([out[0]] + [swap(out[k], "wide", k) for k in range(1, n_wide)])
    beside = swap(owned, "narrow", 1)
    across = swap(owned, "narrow", 2)
    opposite = swap(across, "narrow", 1)
    ids = bag_ids[0].T
    new_table, new_accum = update_part(place, ids, tables[0], accum, [owned, beside, across, opposite])

    half = keep + swap(send, "narrow", 1)
    quarter = half.shape[0] // 2
    mine = lax.dynamic_slice_in_dim(half, chip * quarter, quarter, 0)
    theirs = lax.dynamic_slice_in_dim(half, (1 - chip) * quarter, quarter, 0)
    mine = mine + swap(theirs.astype(jnp.bfloat16), "narrow", 2).astype(jnp.float32)
    hidden = mine.shape[1]
    block = hidden // n_wide
    blocks = jnp.transpose(mine.astype(jnp.bfloat16).reshape(quarter, n_wide, block), (1, 0, 2))
    got = lax.all_to_all(blocks, "wide", 0, 0, tiled=True)
    part = jnp.sum(got.astype(jnp.float32), axis=0) / math.sqrt(total)
    other = swap(part, "narrow", 2)
    low = jnp.where(chip == 0, part, other)
    high = jnp.where(chip == 0, other, part)
    part = jnp.concatenate([low, high], axis=0)
    other = swap(part, "narrow", 1)
    low = jnp.where(core == 0, part, other)
    high = jnp.where(core == 0, other, part)
    w_grad = jnp.concatenate([low, high], axis=0)[:inputs].T
    return (new_table[None], new_accum, w_grad)


def solution(mesh):
    placed = (
        P(("wide", "narrow"), None),
        P(("wide", "narrow"), None, None),
        P(),
        P(),
        P(("wide", "narrow"), None),
        P("wide", None, None),
        P("wide", "narrow", None),
        P("wide", "narrow"),
    )
    return jax.shard_map(
        body,
        mesh=mesh,
        in_specs=placed,
        out_specs=(P("wide", "narrow", None), P("wide", "narrow"), P("wide", None)),
        check_vma=False,
    )
```

```python
import functools
import math

import jax
import jax.numpy as jnp
import numpy as np
from jax import lax
from jax.experimental import pallas as pl
from jax.experimental.pallas import tpu as pltpu
from jax.sharding import PartitionSpec as P

NT = (((1,), (1,)), ((), ()))


def eye(n):
    r = lax.broadcasted_iota(jnp.int32, (n, n), 0)
    c = lax.broadcasted_iota(jnp.int32, (n, n), 1)
    return jnp.where(r == c, 1.0, 0.0).astype(jnp.bfloat16)


def local_kernel(place, dense_in, pooled_in, w_in, bias_in, d_hidden_in, *refs):
    dense, pooled, w_t, bias, d_hidden, pooled32, feat_t, zrows, z_t, dp_t, wg, sems = refs[-12:]
    hold, give, keep, send = refs[:4]
    moves = [
        pltpu.make_async_copy(source, target, sems.at[i])
        for i, (source, target) in enumerate(
            ((pooled_in, pooled), (dense_in, dense), (w_in, w_t), (bias_in, bias), (d_hidden_in, d_hidden))
        )
    ]
    for move in moves:
        move.start()
    samples, width = dense.shape
    tables = pooled.shape[0] // samples
    count = tables + 1
    low_i, low_j = np.tril_indices(count, -1)
    pairs = len(low_i)
    of_pair = {}
    for p, (i, j) in enumerate(zip(low_i, low_j)):
        of_pair[int(i), int(j)] = of_pair[int(j), int(i)] = p
    wide, core = place[0], place[1]

    moves[0].wait()
    for h in range(width // 128):
        pooled32[h] = pooled[:, h * 128 : (h + 1) * 128].astype(jnp.float32)
    ident = eye(width)
    moves[1].wait()
    feat_t[0] = lax.dot_general(ident, dense[...], NT, preferred_element_type=jnp.float32)
    for t in range(tables):
        rows = jnp.concatenate(
            [pooled32[h, pl.ds(t, samples, stride=tables), :] for h in range(width // 128)], axis=1
        ).astype(jnp.bfloat16)
        feat_t[t + 1] = lax.dot_general(ident, rows, NT, preferred_element_type=jnp.float32)

    def products(c, sums):
        f = [feat_t[i, pl.ds(pl.multiple_of(c * 8, 8), 8), :] for i in range(count)]
        return tuple(s + f[i] * f[j] for s, i, j in zip(sums, low_i, low_j))

    zero = jnp.zeros((8, samples), jnp.float32)
    sums = lax.fori_loop(0, width // 8, products, (zero,) * pairs, unroll=4)
    zrows[...] = jnp.zeros_like(zrows)
    for p in range(pairs):
        zrows[p : p + 1, :] = jnp.sum(sums[p], axis=0, keepdims=True)

    z_t[:width, :] = feat_t[0].astype(jnp.bfloat16)
    extra = z_t.shape[0] - width
    z_t[width:, :] = zrows[:extra, :].astype(jnp.bfloat16)
    z_pairs = zrows[...].T[:, :pairs].astype(jnp.bfloat16)
    for move in moves[2:]:
        move.wait()
    w_pairs = w_t[width : width + pairs, :]
    pre = (
        jnp.dot(dense[...], w_t[:width, :], preferred_element_type=jnp.float32)
        + jnp.dot(z_pairs, w_pairs, preferred_element_type=jnp.float32)
        + bias[...]
    )
    sig = 1.0 / (1.0 + jnp.exp(-pre))
    slope = sig * (1.0 + pre * (1.0 - sig))
    dpre = (d_hidden[...].astype(jnp.float32) * slope).astype(jnp.bfloat16)
    dsym = lax.dot_general(w_pairs, dpre, NT, preferred_element_type=jnp.float32)
    dsym = dsym.astype(jnp.bfloat16).astype(jnp.float32)

    spread = [jnp.broadcast_to(dsym[p : p + 1, :], (8, samples)) for p in range(pairs)]

    def gradients(c, carry):
        for h in range(2):
            at = pl.ds(pl.multiple_of(c * 16 + h * 8, 8), 8)
            f = [feat_t[i, at, :] for i in range(count)]
            for t in range(tables):
                total = None
                for g in range(count):
                    if g != t + 1:
                        term = spread[of_pair[t + 1, g]] * f[g]
                        total = term if total is None else total + term
                dp_t[t, at, :] = total
        return carry

    lax.fori_loop(0, width // 16, gradients, 0)
    ident_s = eye(samples)
    for i in range(tables // 2):
        for target, side in ((give, 1 - core), (hold, core)):
            held = dp_t[jnp.bitwise_xor(wide, 2 * i + side)].astype(jnp.bfloat16)
            got = lax.dot_general(ident_s, held, NT, preferred_element_type=jnp.float32)
            target[i] = got.astype(jnp.bfloat16)
    half, block = keep.shape[1:]
    for h in range(2):
        part = jnp.dot(z_t[h * half : (h + 1) * half, :], dpre, preferred_element_type=jnp.float32)
        for b in range(tables):
            wg[h, jnp.bitwise_xor(wide, b)] = part[:, b * block : (b + 1) * block]
    keep[...] = wg[core]
    send[...] = wg[1 - core]


def local_part(place, dense, pooled, w_t, bias, d_hidden):
    samples, width = dense.shape
    tables = pooled.shape[1]
    hidden = w_t.shape[1]
    padded = -(-w_t.shape[0] // 32) * 32
    half = padded // 2
    vmem, hbm = pl.BlockSpec(memory_space=pltpu.VMEM), pl.BlockSpec(memory_space=pltpu.HBM)
    gradients = [(tables // 2, samples, width)] * 2
    operands = (dense, pooled.reshape(samples * tables, width), w_t, bias.reshape(1, hidden), d_hidden)
    return pl.pallas_call(
        local_kernel,
        out_shape=[jax.ShapeDtypeStruct(shape, jnp.bfloat16) for shape in gradients]
        + [jax.ShapeDtypeStruct((tables, half, hidden // tables), jnp.float32)] * 2,
        in_specs=[pl.BlockSpec(memory_space=pltpu.SMEM)] + [hbm] * 5,
        out_specs=[vmem] * (len(gradients) + 2),
        scratch_shapes=[
            pltpu.VMEM((samples, width), dense.dtype),
            pltpu.VMEM((samples * tables, width), pooled.dtype),
            pltpu.VMEM(w_t.shape, w_t.dtype),
            pltpu.VMEM((1, hidden), bias.dtype),
            pltpu.VMEM((samples, hidden), d_hidden.dtype),
            pltpu.VMEM((width // 128, samples * tables, 128), jnp.float32),
            pltpu.VMEM((tables + 1, width, samples), jnp.float32),
            pltpu.VMEM((128, samples), jnp.float32),
            pltpu.VMEM((padded, samples), jnp.bfloat16),
            pltpu.VMEM((tables, width, samples), jnp.float32),
            pltpu.VMEM((2, tables, half, hidden // tables), jnp.float32),
            pltpu.SemaphoreType.DMA((5,)),
        ],
        compiler_params=pltpu.CompilerParams(vmem_limit_bytes=14 * 2**20),
    )(place, *[pltpu.with_memory_space_constraint(x, pltpu.HBM) for x in operands])


def row_kernel(groups, first, last, joined, n_narrow, rows, place, ids, *refs):
    refs = list(refs)
    table_in, accum = (refs.pop(0), refs.pop(0)) if last else (None, None)
    before_in = None if first else refs.pop(0)
    grads = [refs.pop(0) for _ in groups]
    out_sems, sems, done = refs.pop(), refs.pop(), refs.pop()
    loads = []

    def load(source, target):
        move = pltpu.make_async_copy(source, target, sems.at[len(loads)])
        move.start()
        loads.append(move)

    if not first:
        before = refs.pop()
        load(before_in, before)
    if last:
        spread, table = refs.pop(), refs.pop()
        load(table_in, table)
        new_table, new_accum = refs.pop(0), refs.pop(0)
    else:
        sums = refs.pop(0)
        if joined:
            whole, start = refs.pop(0), 0
            for i in joined:
                whole[start : start + grads[i].shape[0]] = grads[i][...]
                start += grads[i].shape[0]
    kept = refs
    wide, core, narrow = place[0], place[1], place[2]
    samples, width = grads[0].shape[1:]
    step, tile, lane = 16, min(512, rows), 128
    down = lax.broadcasted_iota(jnp.int32, (step, samples), 0)
    for pieces, keep in zip(groups, kept):
        for i, (j, k, flip) in enumerate(pieces):
            at = jnp.bitwise_xor(wide, 2 * k + jnp.bitwise_xor(core, flip)) * n_narrow + jnp.bitwise_xor(narrow, j)
            local = ids[:, pl.ds(pl.multiple_of(at * samples, samples), samples)] - narrow * rows
            for s in range(2):
                keep[s, :, i * samples : (i + 1) * samples] = (
                    jnp.broadcast_to(local[s : s + 1, :], (step, samples)) - down
                ).astype(jnp.int16)
    one, none = jnp.bfloat16(1), jnp.bfloat16(0)

    leave = []
    for m in range(rows // tile):
        base = m * tile
        at = slice(base, base + tile)
        total = None
        for grad, keep in zip(grads, kept):
            a, b = keep[0], keep[1]
            parts = []
            for i in range(tile // step):
                want = jnp.int16(base + i * step)
                parts.append(jnp.where(a == want, one, none) + jnp.where(b == want, one, none))
            hot = jnp.concatenate(parts, axis=0)
            term = jnp.dot(hot, grad[...].reshape(-1, width), preferred_element_type=jnp.float32)
            total = term if total is None else total + term
        if not first:
            if m == 0:
                loads[0].wait()
            total = total + before[at, :]
        done[at, :] = total
        if last:
            mean = jnp.sum(total * total, axis=1, keepdims=True) * (1.0 / width)
            spread[at, :] = jnp.broadcast_to(mean, (tile, lane))
        else:
            out = pltpu.make_async_copy(done.at[at, :], sums.at[at, :], out_sems.at[m])
            out.start()
            leave.append(out)
    if not last:
        for out in leave:
            out.wait()
        return
    parts = [slice(i * lane, (i + 1) * lane) for i in range(rows // lane)]
    mean = jnp.concatenate([spread[part, :].T[:1, :] for part in parts], axis=1)
    fresh = accum[...] + mean
    new_accum[...] = fresh
    rate = 0.1 / (jnp.sqrt(fresh) + 1e-8)
    loads[-1].wait()
    for i, part in enumerate(parts):
        by_row = jnp.broadcast_to(rate[:, part], (lane, lane)).T
        for h in range(width // lane):
            cols = slice(h * lane, (h + 1) * lane)
            table[part, cols] = table[part, cols] - done[part, cols] * by_row
        out = pltpu.make_async_copy(table.at[part, :], new_table.at[part, :], out_sems.at[i])
        out.start()
        leave.append(out)
    for out in leave:
        out.wait()


def row_part(groups, place, ids, grads, rows, n_narrow, before=None, table=None, accum=None, joined=()):
    samples, width = grads[0].shape[1:]
    first, last = before is None, table is not None
    vmem, hbm = pl.BlockSpec(memory_space=pltpu.VMEM), pl.BlockSpec(memory_space=pltpu.HBM)
    operands = ([table, accum] if last else []) + ([] if first else [before]) + list(grads)
    sums = jax.ShapeDtypeStruct((rows, width), jnp.float32)
    if last:
        out_shape = (sums, jax.ShapeDtypeStruct((1, rows), jnp.float32))
    elif joined:
        out_shape = (sums, jax.ShapeDtypeStruct((sum(len(groups[i]) for i in joined), samples, width), grads[0].dtype))
    else:
        out_shape = (sums,)
    scratch = [pltpu.VMEM((2, 16, len(pieces) * samples), jnp.int16) for pieces in groups]
    whole = pltpu.VMEM((rows, width), jnp.float32)
    if last:
        scratch += [whole, pltpu.VMEM((rows, 128), jnp.float32)]
    if not first:
        scratch += [whole]
    scratch += [whole, pltpu.SemaphoreType.DMA((2,)), pltpu.SemaphoreType.DMA((rows // 128,))]
    return pl.pallas_call(
        functools.partial(row_kernel, groups, first, last, joined, n_narrow, rows),
        out_shape=out_shape,
        in_specs=[pl.BlockSpec(memory_space=pltpu.SMEM), vmem]
        + ([hbm, vmem] if last else [])
        + ([] if first else [hbm])
        + [vmem] * len(grads),
        out_specs=(hbm, vmem)[: len(out_shape)],
        scratch_shapes=scratch,
        compiler_params=pltpu.CompilerParams(vmem_limit_bytes=14 * 2**20),
        cost_estimate=pl.CostEstimate(
            flops=2 * rows * samples * width * sum(len(pieces) for pieces in groups),
            bytes_accessed=8 * rows * width,
            transcendentals=0,
        ),
    )(place, ids, *operands)


def row_sums(grads, ids, offset, count):
    local = ids - offset
    local = jnp.where((local >= 0) & (local < count), local, count)
    result = jnp.zeros((count, grads.shape[1]), jnp.float32)
    for slot in range(ids.shape[1]):
        result = result + jax.ops.segment_sum(grads, local[:, slot], num_segments=count + 1)[:count]
    return result


def plain_body(dense, pooled, w_top, bias, d_hidden, bag_ids, tables, accum):
    samples = dense.shape[0]
    width = dense.shape[1]
    n_wide = lax.axis_size("wide")
    n_narrow = lax.axis_size("narrow")
    total = samples * n_wide * n_narrow
    feats = jnp.concatenate([dense[:, None, :], pooled], axis=1)
    count = feats.shape[1]
    low_i, low_j = np.tril_indices(count, -1)
    zmat = jnp.einsum("bfd,bgd->bfg", feats, feats, preferred_element_type=jnp.float32)
    z_in = jnp.concatenate([dense.astype(jnp.float32), zmat[:, low_i, low_j]], axis=1).astype(
        jnp.bfloat16
    )
    pre = jnp.dot(z_in, w_top.T, preferred_element_type=jnp.float32) + bias
    sig = jax.nn.sigmoid(pre)
    slope = sig * (1.0 + pre * (1.0 - sig))
    dpre = (d_hidden.astype(jnp.float32) * slope).astype(jnp.bfloat16)
    dz_full = jnp.dot(dpre, w_top, preferred_element_type=jnp.float32)
    dpairs = dz_full[:, width:]
    dmat = jnp.zeros((samples, count * count), jnp.float32).at[:, low_i * count + low_j].set(dpairs)
    dmat = dmat.reshape(samples, count, count)
    dsym = (dmat + jnp.transpose(dmat, (0, 2, 1))).astype(jnp.bfloat16)
    dfeat = jnp.einsum("bfg,bgd->bfd", dsym, feats, preferred_element_type=jnp.float32)
    dpooled = dfeat[:, 1:, :].astype(jnp.bfloat16)
    part = lax.slice_in_dim(dpre, 0, w_top.shape[0] // n_wide * lax.axis_size("wide"), axis=1)
    wide_part = lax.psum_scatter(
        jnp.dot(part.T, z_in, preferred_element_type=jnp.float32),
        "wide",
        scatter_dimension=0,
        tiled=True,
    )
    w_grad = lax.psum(wide_part, "narrow") / math.sqrt(total)
    owned = lax.all_to_all(dpooled, "wide", split_axis=1, concat_axis=0, tiled=True).reshape(
        n_wide * samples, width
    )
    bag = bag_ids.shape[2]
    ids_four = bag_ids[0].reshape(n_wide, n_narrow, samples, bag)
    rows_dev = tables.shape[1]
    narrow_pos = lax.axis_index("narrow")
    every = lax.all_gather(owned, "narrow", axis=0, tiled=True)
    ids_all = jnp.transpose(ids_four, (1, 0, 2, 3)).reshape(-1, bag)
    row_grad = row_sums(every.astype(jnp.float32), ids_all, narrow_pos * rows_dev, rows_dev)
    acc_new = accum[0] + jnp.mean(row_grad * row_grad, axis=1)
    table_new = tables[0] - 0.1 * row_grad / (jnp.sqrt(acc_new)[:, None] + 1e-08)
    return (table_new[None], acc_new[None], w_grad)


def body(dense, pooled, w_top, bias, d_hidden, bag_ids, tables, accum):
    n_wide, n_narrow = lax.axis_size("wide"), lax.axis_size("narrow")
    samples, count = dense.shape[0], pooled.shape[1]
    rows, width = tables.shape[1:]
    inputs = w_top.shape[1]
    total = samples * n_wide * n_narrow
    if n_narrow != 4 or n_wide & (n_wide - 1) or count != n_wide or total * width > 2**21:
        return plain_body(dense, pooled, w_top, bias, d_hidden, bag_ids, tables, accum)
    wide, narrow = lax.axis_index("wide"), lax.axis_index("narrow")
    core, chip = narrow % 2, narrow // 2
    place = jnp.stack([wide, core, narrow]).astype(jnp.int32)

    def swap(array, axis, bit):
        n = lax.axis_size(axis)
        return lax.ppermute(array, axis, [(i, i ^ bit) for i in range(n)])

    out = local_part(place, dense, pooled, w_top.T, bias, d_hidden)
    hold, give, keep, send = out
    ids = bag_ids[0].T
    tie = lambda *values: lax.optimization_barrier(values)
    taken = swap(give, "narrow", 1)
    received = swap(send, "narrow", 1)

    def reach(i):
        lead = jnp.stack([hold[i], taken[i]])
        pairs = [
            (w * n_narrow + n, (w ^ (2 * i + n % 2)) * n_narrow + n) for w in range(n_wide) for n in range(n_narrow)
        ]
        return lax.ppermute(lead, ("wide", "narrow"), pairs)

    got = {i: reach(i) for i in (1, 0, 2, 3)}
    got[0], got[1], received = tie(got[0], got[1], received)
    half = keep + received
    half_y = swap(half[1::2].astype(jnp.bfloat16), "wide", 1)
    near = jnp.concatenate([got[0], got[1]])
    across_near = swap(near, "narrow", 2)
    half = half[0::2] + half_y.astype(jnp.float32)
    half_z = swap(half[1::2].astype(jnp.bfloat16), "wide", 2)
    got[2], got[3], half_z, across_near = tie(got[2], got[3], half_z, across_near)
    far = jnp.concatenate([got[2], got[3]])
    across_far = swap(far, "narrow", 2)
    half = half[0::2] + half_z.astype(jnp.float32)
    half_zz = swap(half[1::2].astype(jnp.bfloat16), "wide", 4)
    mine = jnp.concatenate([near, far])
    beside = swap(mine, "narrow", 1)
    across_far, half_zz = tie(across_far, half_zz)
    across = jnp.concatenate([across_near, across_far])
    opposite = swap(across, "narrow", 1)
    half = half[0::2] + half_zz.astype(jnp.float32)
    part = half[0] / math.sqrt(total)
    part_x = swap(part, "narrow", 2)
    opposite, part_x = tie(opposite, part_x)
    part = part + part_x
    other = swap(part, "narrow", 1)
    pieces = lambda j, flip: tuple((j ^ s, i, flip) for i in range(n_wide // 2) for s in range(2))
    new_table, new_accum = row_part(
        [pieces(0, 0), pieces(1, 1), pieces(2, 0), pieces(3, 1)],
        place, ids, [mine, beside, across, opposite], rows, n_narrow, table=tables[0], accum=accum,
    )
    other, new_accum = tie(other, new_accum)
    low = jnp.where(core == 0, part, other)
    high = jnp.where(core == 0, other, part)
    w_grad = jnp.concatenate([low, high], axis=0)[:inputs].T
    return (new_table[None], new_accum, w_grad)


def solution(mesh):
    placed = (
        P(("wide", "narrow"), None),
        P(("wide", "narrow"), None, None),
        P(),
        P(),
        P(("wide", "narrow"), None),
        P("wide", None, None),
        P("wide", "narrow", None),
        P("wide", "narrow"),
    )
    return jax.shard_map(
        body,
        mesh=mesh,
        in_specs=placed,
        out_specs=(P("wide", "narrow", None), P("wide", "narrow"), P("wide", None)),
        check_vma=False,
    )
```

```python
import functools
import math

import jax
import jax.numpy as jnp
import numpy as np
from jax import lax
from jax.experimental import pallas as pl
from jax.experimental.pallas import tpu as pltpu
from jax.sharding import PartitionSpec as P

NT = (((1,), (1,)), ((), ()))


def eye(n):
    r = lax.broadcasted_iota(jnp.int32, (n, n), 0)
    c = lax.broadcasted_iota(jnp.int32, (n, n), 1)
    return jnp.where(r == c, 1.0, 0.0).astype(jnp.bfloat16)


def local_kernel(place, dense_in, pooled_in, w_in, bias_in, d_hidden_in, *refs):
    dense, pooled, w_t, bias, d_hidden, pooled32, feat_t, zrows, z_t, dp_t, sems = refs[-11:]
    hold, give, keep, send = refs[:4]
    moves = [
        pltpu.make_async_copy(source, target, sems.at[i])
        for i, (source, target) in enumerate(
            ((pooled_in, pooled), (dense_in, dense), (w_in, w_t), (bias_in, bias), (d_hidden_in, d_hidden))
        )
    ]
    for move in moves:
        move.start()
    samples, width = dense.shape
    tables = pooled.shape[0] // samples
    count = tables + 1
    low_i, low_j = np.tril_indices(count, -1)
    pairs = len(low_i)
    of_pair = {}
    for p, (i, j) in enumerate(zip(low_i, low_j)):
        of_pair[int(i), int(j)] = of_pair[int(j), int(i)] = p
    wide, core = place[0], place[1]

    moves[0].wait()
    for h in range(width // 128):
        pooled32[h] = pooled[:, h * 128 : (h + 1) * 128].astype(jnp.float32)
    ident = eye(width)
    moves[1].wait()
    feat_t[0] = lax.dot_general(ident, dense[...], NT, preferred_element_type=jnp.float32)
    for t in range(tables):
        rows = jnp.concatenate(
            [pooled32[h, pl.ds(t, samples, stride=tables), :] for h in range(width // 128)], axis=1
        ).astype(jnp.bfloat16)
        feat_t[t + 1] = lax.dot_general(ident, rows, NT, preferred_element_type=jnp.float32)

    def products(c, sums):
        f = [feat_t[i, pl.ds(pl.multiple_of(c * 8, 8), 8), :] for i in range(count)]
        return tuple(s + f[i] * f[j] for s, i, j in zip(sums, low_i, low_j))

    zero = jnp.zeros((8, samples), jnp.float32)
    sums = lax.fori_loop(0, width // 8, products, (zero,) * pairs, unroll=4)
    zrows[...] = jnp.zeros_like(zrows)
    for p in range(pairs):
        zrows[p : p + 1, :] = jnp.sum(sums[p], axis=0, keepdims=True)

    z_t[:width, :] = feat_t[0].astype(jnp.bfloat16)
    extra = z_t.shape[0] - width
    z_t[width:, :] = zrows[:extra, :].astype(jnp.bfloat16)
    z_pairs = zrows[...].T[:, :pairs].astype(jnp.bfloat16)
    for move in moves[2:]:
        move.wait()
    w_pairs = w_t[width : width + pairs, :]
    pre = (
        jnp.dot(dense[...], w_t[:width, :], preferred_element_type=jnp.float32)
        + jnp.dot(z_pairs, w_pairs, preferred_element_type=jnp.float32)
        + bias[...]
    )
    sig = 1.0 / (1.0 + jnp.exp(-pre))
    slope = sig * (1.0 + pre * (1.0 - sig))
    dpre = (d_hidden[...].astype(jnp.float32) * slope).astype(jnp.bfloat16)
    dsym = lax.dot_general(w_pairs, dpre, NT, preferred_element_type=jnp.float32)
    dsym = dsym.astype(jnp.bfloat16).astype(jnp.float32)

    spread = [jnp.broadcast_to(dsym[p : p + 1, :], (8, samples)) for p in range(pairs)]

    def gradients(c, carry):
        for h in range(2):
            at = pl.ds(pl.multiple_of(c * 16 + h * 8, 8), 8)
            f = [feat_t[i, at, :] for i in range(count)]
            for t in range(tables):
                total = None
                for g in range(count):
                    if g != t + 1:
                        term = spread[of_pair[t + 1, g]] * f[g]
                        total = term if total is None else total + term
                dp_t[t, at, :] = total
        return carry

    lax.fori_loop(0, width // 16, gradients, 0, unroll=2)
    ident_s = eye(samples)
    for i in range(tables // 2):
        for target, side in ((give, 1 - core), (hold, core)):
            held = dp_t[jnp.bitwise_xor(wide, 2 * i + side)].astype(jnp.bfloat16)
            got = lax.dot_general(ident_s, held, NT, preferred_element_type=jnp.float32)
            target[i] = got.astype(jnp.bfloat16)
    half, block = keep.shape[1:]
    for target, side in ((send, 1 - core), (keep, core)):
        mine = z_t[pl.ds(pl.multiple_of(side * half, 16), half), :]
        part = jnp.dot(mine, dpre, preferred_element_type=jnp.float32)
        for b in range(tables):
            target[jnp.bitwise_xor(wide, b)] = part[:, b * block : (b + 1) * block]


def local_part(place, dense, pooled, w_t, bias, d_hidden):
    samples, width = dense.shape
    tables = pooled.shape[1]
    hidden = w_t.shape[1]
    padded = -(-w_t.shape[0] // 32) * 32
    half = padded // 2
    vmem, hbm = pl.BlockSpec(memory_space=pltpu.VMEM), pl.BlockSpec(memory_space=pltpu.HBM)
    gradients = [(tables // 2, samples, width)] * 2
    operands = (dense, pooled.reshape(samples * tables, width), w_t, bias.reshape(1, hidden), d_hidden)
    return pl.pallas_call(
        local_kernel,
        out_shape=[jax.ShapeDtypeStruct(shape, jnp.bfloat16) for shape in gradients]
        + [jax.ShapeDtypeStruct((tables, half, hidden // tables), jnp.float32)] * 2,
        in_specs=[pl.BlockSpec(memory_space=pltpu.SMEM)] + [hbm] * 5,
        out_specs=[vmem] * (len(gradients) + 2),
        scratch_shapes=[
            pltpu.VMEM((samples, width), dense.dtype),
            pltpu.VMEM((samples * tables, width), pooled.dtype),
            pltpu.VMEM(w_t.shape, w_t.dtype),
            pltpu.VMEM((1, hidden), bias.dtype),
            pltpu.VMEM((samples, hidden), d_hidden.dtype),
            pltpu.VMEM((width // 128, samples * tables, 128), jnp.float32),
            pltpu.VMEM((tables + 1, width, samples), jnp.float32),
            pltpu.VMEM((128, samples), jnp.float32),
            pltpu.VMEM((padded, samples), jnp.bfloat16),
            pltpu.VMEM((tables, width, samples), jnp.float32),
            pltpu.SemaphoreType.DMA((5,)),
        ],
        compiler_params=pltpu.CompilerParams(vmem_limit_bytes=14 * 2**20),
    )(place, *[pltpu.with_memory_space_constraint(x, pltpu.HBM) for x in operands])


def row_kernel(groups, n_narrow, place, ids, table_in, accum, *refs):
    count = len(groups)
    grads, (new_table, new_accum), kept = refs[:count], refs[count : count + 2], refs[count + 2 : 2 * count + 2]
    table, fresh_out, done, spread, sems = refs[2 * count + 2 :]
    arrive = pltpu.make_async_copy(table_in, table, sems.at[0])
    arrive.start()
    wide, core, narrow = place[0], place[1], place[2]
    samples, width = grads[0].shape[1:]
    rows = table.shape[0]
    step, tile, lane = 16, min(256, rows), 128
    down = lax.broadcasted_iota(jnp.int32, (step, samples), 0)
    for pieces, keep in zip(groups, kept):
        for i, (j, k, flip) in enumerate(pieces):
            at = jnp.bitwise_xor(wide, 2 * k + jnp.bitwise_xor(core, flip)) * n_narrow + jnp.bitwise_xor(narrow, j)
            local = ids[:, pl.ds(pl.multiple_of(at * samples, samples), samples)] - narrow * rows
            for s in range(2):
                keep[s, :, i * samples : (i + 1) * samples] = (
                    jnp.broadcast_to(local[s : s + 1, :], (step, samples)) - down
                ).astype(jnp.int16)
    one, none = jnp.bfloat16(1), jnp.bfloat16(0)
    leave = []
    for base in range(0, rows, tile):
        total = None
        for grad, keep in zip(grads, kept):
            a, b = keep[0], keep[1]
            parts = []
            for i in range(tile // step):
                want = jnp.int16(base + i * step)
                parts.append(jnp.where(a == want, one, none) + jnp.where(b == want, one, none))
            hot = jnp.concatenate(parts, axis=0)
            term = jnp.dot(hot, grad[...].reshape(-1, width), preferred_element_type=jnp.float32)
            total = term if total is None else total + term
        at = slice(base, base + tile)
        done[at, :] = total
        mean = jnp.sum(total * total, axis=1, keepdims=True) * (1.0 / width)
        spread[at, :] = jnp.broadcast_to(mean, (tile, lane))
    cuts = [slice(start, start + lane) for start in range(0, rows, lane)]
    fresh_out[...] = accum[...] + jnp.concatenate([spread[cut, :].T[:1, :] for cut in cuts], axis=1)

    def depart(source, target):
        move = pltpu.make_async_copy(source, target, sems.at[1 + len(leave)])
        move.start()
        leave.append(move)

    depart(fresh_out, new_accum)
    rate = 0.1 / (jnp.sqrt(fresh_out[...]) + 1e-8)
    arrive.wait()
    for cut in cuts:
        by_row = jnp.broadcast_to(rate[:, cut], (lane, lane)).T
        for h in range(width // lane):
            cols = slice(h * lane, (h + 1) * lane)
            table[cut, cols] = table[cut, cols] - done[cut, cols] * by_row
        depart(table.at[cut, :], new_table.at[cut, :])
    for move in leave:
        move.wait()


def row_part(groups, place, ids, grads, n_narrow, table, accum):
    rows, width = table.shape
    samples = grads[0].shape[1]
    vmem, hbm = pl.BlockSpec(memory_space=pltpu.VMEM), pl.BlockSpec(memory_space=pltpu.HBM)
    return pl.pallas_call(
        functools.partial(row_kernel, groups, n_narrow),
        out_shape=(
            jax.ShapeDtypeStruct((rows, width), jnp.float32),
            jax.ShapeDtypeStruct((1, rows), jnp.float32),
        ),
        in_specs=[pl.BlockSpec(memory_space=pltpu.SMEM), vmem, hbm, vmem] + [vmem] * len(grads),
        out_specs=(hbm, hbm),
        scratch_shapes=[pltpu.VMEM((2, 16, len(pieces) * samples), jnp.int16) for pieces in groups]
        + [
            pltpu.VMEM((rows, width), jnp.float32),
            pltpu.VMEM((1, rows), jnp.float32),
            pltpu.VMEM((rows, width), jnp.float32),
            pltpu.VMEM((rows, 128), jnp.float32),
            pltpu.SemaphoreType.DMA((2 + rows // 128,)),
        ],
        compiler_params=pltpu.CompilerParams(vmem_limit_bytes=14 * 2**20),
        cost_estimate=pl.CostEstimate(
            flops=2 * rows * samples * width * sum(len(pieces) for pieces in groups),
            bytes_accessed=8 * rows * width,
            transcendentals=0,
        ),
    )(place, ids, table, accum, *grads)


def row_sums(grads, ids, offset, count):
    local = ids - offset
    local = jnp.where((local >= 0) & (local < count), local, count)
    result = jnp.zeros((count, grads.shape[1]), jnp.float32)
    for slot in range(ids.shape[1]):
        result = result + jax.ops.segment_sum(grads, local[:, slot], num_segments=count + 1)[:count]
    return result


def plain_body(dense, pooled, w_top, bias, d_hidden, bag_ids, tables, accum):
    samples = dense.shape[0]
    width = dense.shape[1]
    n_wide = lax.axis_size("wide")
    n_narrow = lax.axis_size("narrow")
    total = samples * n_wide * n_narrow
    feats = jnp.concatenate([dense[:, None, :], pooled], axis=1)
    count = feats.shape[1]
    low_i, low_j = np.tril_indices(count, -1)
    zmat = jnp.einsum("bfd,bgd->bfg", feats, feats, preferred_element_type=jnp.float32)
    z_in = jnp.concatenate([dense.astype(jnp.float32), zmat[:, low_i, low_j]], axis=1).astype(
        jnp.bfloat16
    )
    pre = jnp.dot(z_in, w_top.T, preferred_element_type=jnp.float32) + bias
    sig = jax.nn.sigmoid(pre)
    slope = sig * (1.0 + pre * (1.0 - sig))
    dpre = (d_hidden.astype(jnp.float32) * slope).astype(jnp.bfloat16)
    dz_full = jnp.dot(dpre, w_top, preferred_element_type=jnp.float32)
    dpairs = dz_full[:, width:]
    dmat = jnp.zeros((samples, count * count), jnp.float32).at[:, low_i * count + low_j].set(dpairs)
    dmat = dmat.reshape(samples, count, count)
    dsym = (dmat + jnp.transpose(dmat, (0, 2, 1))).astype(jnp.bfloat16)
    dfeat = jnp.einsum("bfg,bgd->bfd", dsym, feats, preferred_element_type=jnp.float32)
    dpooled = dfeat[:, 1:, :].astype(jnp.bfloat16)
    part = lax.slice_in_dim(dpre, 0, w_top.shape[0] // n_wide * lax.axis_size("wide"), axis=1)
    wide_part = lax.psum_scatter(
        jnp.dot(part.T, z_in, preferred_element_type=jnp.float32),
        "wide",
        scatter_dimension=0,
        tiled=True,
    )
    w_grad = lax.psum(wide_part, "narrow") / math.sqrt(total)
    owned = lax.all_to_all(dpooled, "wide", split_axis=1, concat_axis=0, tiled=True).reshape(
        n_wide * samples, width
    )
    bag = bag_ids.shape[2]
    ids_four = bag_ids[0].reshape(n_wide, n_narrow, samples, bag)
    rows_dev = tables.shape[1]
    narrow_pos = lax.axis_index("narrow")
    every = lax.all_gather(owned, "narrow", axis=0, tiled=True)
    ids_all = jnp.transpose(ids_four, (1, 0, 2, 3)).reshape(-1, bag)
    row_grad = row_sums(every.astype(jnp.float32), ids_all, narrow_pos * rows_dev, rows_dev)
    acc_new = accum[0] + jnp.mean(row_grad * row_grad, axis=1)
    table_new = tables[0] - 0.1 * row_grad / (jnp.sqrt(acc_new)[:, None] + 1e-08)
    return (table_new[None], acc_new[None], w_grad)


def body(dense, pooled, w_top, bias, d_hidden, bag_ids, tables, accum):
    n_wide, n_narrow = lax.axis_size("wide"), lax.axis_size("narrow")
    samples, count = dense.shape[0], pooled.shape[1]
    rows, width = tables.shape[1:]
    inputs = w_top.shape[1]
    total = samples * n_wide * n_narrow
    if n_narrow != 4 or n_wide & (n_wide - 1) or count != n_wide or total * width > 2**21:
        return plain_body(dense, pooled, w_top, bias, d_hidden, bag_ids, tables, accum)
    wide, narrow = lax.axis_index("wide"), lax.axis_index("narrow")
    core, chip = narrow % 2, narrow // 2
    place = jnp.stack([wide, core, narrow]).astype(jnp.int32)

    def swap(array, axis, bit):
        n = lax.axis_size(axis)
        return lax.ppermute(array, axis, [(i, i ^ bit) for i in range(n)])

    out = local_part(place, dense, pooled, w_top.T, bias, d_hidden)
    hold, give, keep, send = out
    ids = bag_ids[0].T
    tie = lambda *values: lax.optimization_barrier(values)
    taken = swap(give, "narrow", 1)
    received = swap(send, "narrow", 1)

    def reach(i):
        lead = jnp.stack([hold[i], taken[i]])
        pairs = [
            (w * n_narrow + n, (w ^ (2 * i + n % 2)) * n_narrow + n) for w in range(n_wide) for n in range(n_narrow)
        ]
        return lax.ppermute(lead, ("wide", "narrow"), pairs)

    got = {i: reach(i) for i in (1, 0, 2, 3)}
    got[0], got[1], received = tie(got[0], got[1], received)
    half = keep + received
    half_y = swap(half[1::2].astype(jnp.bfloat16), "wide", 1)
    near = jnp.concatenate([got[0], got[1]])
    across_near = swap(near, "narrow", 2)
    got[2], got[3], across_near = tie(got[2], got[3], across_near)
    far = jnp.concatenate([got[2], got[3]])
    across_far = swap(far, "narrow", 2)
    half = half[0::2] + half_y.astype(jnp.float32)
    columns = [swap(half[i].astype(jnp.bfloat16), "wide", 2 * i) for i in range(1, n_wide // 2)]
    mine = jnp.concatenate([near, far])
    beside = swap(mine, "narrow", 1)
    across_far, *columns = tie(across_far, *columns)
    across = jnp.concatenate([across_near, across_far])
    opposite = swap(across, "narrow", 1)
    part = sum([column.astype(jnp.float32) for column in columns], half[0]) / math.sqrt(total)
    others = [swap(part, "narrow", bit) for bit in (1, 2, 3)]
    pieces = lambda j, flip: tuple((j ^ s, i, flip) for i in range(n_wide // 2) for s in range(2))
    new_table, new_accum = row_part(
        [pieces(0, 0), pieces(1, 1), pieces(2, 0), pieces(3, 1)],
        place, ids, [mine, beside, across, opposite], n_narrow, tables[0], accum,
    )
    others[0], others[1], others[2], new_accum = tie(*others, new_accum)
    part, other = part + others[1], others[0] + others[2]
    low = jnp.where(core == 0, part, other)
    high = jnp.where(core == 0, other, part)
    w_grad = jnp.concatenate([low, high], axis=0)[:inputs].T
    return (new_table[None], new_accum, w_grad)


def solution(mesh):
    placed = (
        P(("wide", "narrow"), None),
        P(("wide", "narrow"), None, None),
        P(),
        P(),
        P(("wide", "narrow"), None),
        P("wide", None, None),
        P("wide", "narrow", None),
        P("wide", "narrow"),
    )
    return jax.shard_map(
        body,
        mesh=mesh,
        in_specs=placed,
        out_specs=(P("wide", "narrow", None), P("wide", "narrow"), P("wide", None)),
        check_vma=False,
    )
```

```python
import functools
import math

import jax
import jax.numpy as jnp
import numpy as np
from jax import lax
from jax.experimental import pallas as pl
from jax.experimental.pallas import tpu as pltpu
from jax.sharding import PartitionSpec as P

NT = (((1,), (1,)), ((), ()))


def eye(n):
    r = lax.broadcasted_iota(jnp.int32, (n, n), 0)
    c = lax.broadcasted_iota(jnp.int32, (n, n), 1)
    return jnp.where(r == c, 1.0, 0.0).astype(jnp.bfloat16)


def local_kernel(place, dense_in, pooled_in, w_in, bias_in, d_hidden_in, *refs):
    dense, pooled, w_t, bias, d_hidden, pooled32, feat_t, zrows, z_t, dp_t, dpre_all, sems = refs[-12:]
    hold, give, keep, send = refs[:4]
    moves = [
        pltpu.make_async_copy(source, target, sems.at[i])
        for i, (source, target) in enumerate(
            ((pooled_in, pooled), (dense_in, dense), (w_in, w_t), (bias_in, bias), (d_hidden_in, d_hidden))
        )
    ]
    for move in moves:
        move.start()
    samples, width = dense.shape
    tables = pooled.shape[0] // samples
    count = tables + 1
    low_i, low_j = np.tril_indices(count, -1)
    pairs = len(low_i)
    of_pair = {}
    for p, (i, j) in enumerate(zip(low_i, low_j)):
        of_pair[int(i), int(j)] = of_pair[int(j), int(i)] = p
    wide, core = place[0], place[1]

    moves[0].wait()
    for h in range(width // 128):
        pooled32[h] = pooled[:, h * 128 : (h + 1) * 128].astype(jnp.float32)
    ident = eye(width)
    moves[1].wait()
    feat_t[0] = lax.dot_general(ident, dense[...], NT, preferred_element_type=jnp.float32)
    for t in range(tables):
        rows = jnp.concatenate(
            [pooled32[h, pl.ds(t, samples, stride=tables), :] for h in range(width // 128)], axis=1
        ).astype(jnp.bfloat16)
        feat_t[t + 1] = lax.dot_general(ident, rows, NT, preferred_element_type=jnp.float32)

    def products(c, sums):
        f = [feat_t[i, pl.ds(pl.multiple_of(c * 8, 8), 8), :] for i in range(count)]
        return tuple(s + f[i] * f[j] for s, i, j in zip(sums, low_i, low_j))

    zero = jnp.zeros((8, samples), jnp.float32)
    sums = lax.fori_loop(0, width // 8, products, (zero,) * pairs, unroll=True)
    zrows[...] = jnp.zeros_like(zrows)
    for p in range(pairs):
        zrows[p : p + 1, :] = jnp.sum(sums[p], axis=0, keepdims=True)

    z_t[:width, :] = feat_t[0].astype(jnp.bfloat16)
    extra = z_t.shape[0] - width
    z_t[width:, :] = zrows[:extra, :].astype(jnp.bfloat16)
    z_pairs = zrows[...].T[:, :pairs].astype(jnp.bfloat16)
    for move in moves[2:]:
        move.wait()
    w_pairs = w_t[width : width + pairs, :]
    pre = (
        jnp.dot(dense[...], w_t[:width, :], preferred_element_type=jnp.float32)
        + jnp.dot(z_pairs, w_pairs, preferred_element_type=jnp.float32)
        + bias[...]
    )
    sig = 1.0 / (1.0 + jnp.exp(-pre))
    slope = sig * (1.0 + pre * (1.0 - sig))
    dpre = (d_hidden[...].astype(jnp.float32) * slope).astype(jnp.bfloat16)
    dsym = lax.dot_general(w_pairs, dpre, NT, preferred_element_type=jnp.float32)
    dsym = dsym.astype(jnp.bfloat16).astype(jnp.float32)

    spread = [jnp.broadcast_to(dsym[p : p + 1, :], (8, samples)) for p in range(pairs)]

    def gradients(c, carry):
        for h in range(2):
            at = pl.ds(pl.multiple_of(c * 16 + h * 8, 8), 8)
            f = [feat_t[i, at, :] for i in range(count)]
            for t in range(tables):
                total = None
                for g in range(count):
                    if g != t + 1:
                        term = spread[of_pair[t + 1, g]] * f[g]
                        total = term if total is None else total + term
                dp_t[t, at, :] = total
        return carry

    lax.fori_loop(0, width // 16, gradients, 0, unroll=True)
    ident_s = eye(samples)
    for i in range(tables // 2):
        for target, side in ((give, 1 - core), (hold, core)):
            held = dp_t[jnp.bitwise_xor(wide, 2 * i + jnp.bitwise_xor(side, i % 2))].astype(jnp.bfloat16)
            got = lax.dot_general(ident_s, held, NT, preferred_element_type=jnp.float32)
            target[i] = got.astype(jnp.bfloat16)
    block = keep.shape[2]
    dpre_all[...] = dpre
    for i in range(tables // 2):
        for target, side in ((send, 1 - core), (keep, core)):
            column = jnp.bitwise_xor(wide, 2 * i + jnp.bitwise_xor(side, i % 2)) * block
            mine = dpre_all[:, pl.ds(pl.multiple_of(column, block), block)]
            target[i] = jnp.dot(z_t[...], mine, preferred_element_type=jnp.float32)


def local_part(place, dense, pooled, w_t, bias, d_hidden):
    samples, width = dense.shape
    tables = pooled.shape[1]
    hidden = w_t.shape[1]
    padded = -(-w_t.shape[0] // 16) * 16
    vmem, hbm = pl.BlockSpec(memory_space=pltpu.VMEM), pl.BlockSpec(memory_space=pltpu.HBM)
    gradients = [(tables // 2, samples, width)] * 2
    operands = (dense, pooled.reshape(samples * tables, width), w_t, bias.reshape(1, hidden), d_hidden)
    return pl.pallas_call(
        local_kernel,
        out_shape=[jax.ShapeDtypeStruct(shape, jnp.bfloat16) for shape in gradients]
        + [jax.ShapeDtypeStruct((tables // 2, padded, hidden // tables), jnp.float32)] * 2,
        in_specs=[pl.BlockSpec(memory_space=pltpu.SMEM)] + [hbm] * 5,
        out_specs=[vmem] * (len(gradients) + 2),
        scratch_shapes=[
            pltpu.VMEM((samples, width), dense.dtype),
            pltpu.VMEM((samples * tables, width), pooled.dtype),
            pltpu.VMEM(w_t.shape, w_t.dtype),
            pltpu.VMEM((1, hidden), bias.dtype),
            pltpu.VMEM((samples, hidden), d_hidden.dtype),
            pltpu.VMEM((width // 128, samples * tables, 128), jnp.float32),
            pltpu.VMEM((tables + 1, width, samples), jnp.float32),
            pltpu.VMEM((128, samples), jnp.float32),
            pltpu.VMEM((padded, samples), jnp.bfloat16),
            pltpu.VMEM((tables, width, samples), jnp.float32),
            pltpu.VMEM((samples, hidden), jnp.bfloat16),
            pltpu.SemaphoreType.DMA((5,)),
        ],
        compiler_params=pltpu.CompilerParams(vmem_limit_bytes=14 * 2**20),
    )(place, *[pltpu.with_memory_space_constraint(x, pltpu.HBM) for x in operands])


def bag_rows(groups, n_narrow, place, ids, kept, rows):
    wide, core, narrow = place[0], place[1], place[2]
    step = kept[0].shape[1]
    samples = kept[0].shape[2] // len(groups[0])
    down = lax.broadcasted_iota(jnp.int32, (step, samples), 0)
    for pieces, keep in zip(groups, kept):
        for i, (j, k, flip) in enumerate(pieces):
            source = jnp.bitwise_xor(wide, 2 * k + jnp.bitwise_xor(core, (flip + k) % 2))
            at = source * n_narrow + jnp.bitwise_xor(narrow, j)
            local = ids[:, pl.ds(pl.multiple_of(at * samples, samples), samples)] - narrow * rows
            for s in range(2):
                keep[s, :, i * samples : (i + 1) * samples] = (
                    jnp.broadcast_to(local[s : s + 1, :], (step, samples)) - down
                ).astype(jnp.int16)


def tile_sums(base, tile, grads, kept, width):
    one, none = jnp.bfloat16(1), jnp.bfloat16(0)
    step = kept[0].shape[1]
    total = None
    for grad, keep in zip(grads, kept):
        a, b = keep[0], keep[1]
        parts = []
        for i in range(tile // step):
            want = jnp.int16(base + i * step)
            parts.append(jnp.where(a == want, one, none) + jnp.where(b == want, one, none))
        hot = jnp.concatenate(parts, axis=0)
        term = jnp.dot(hot, grad[...].reshape(-1, width), preferred_element_type=jnp.float32)
        total = term if total is None else total + term
    return total


def early_kernel(groups, n_narrow, place, ids, *refs):
    count = len(groups)
    grads, sums, kept = refs[:count], refs[count], refs[count + 1 :]
    rows, width = sums.shape
    bag_rows(groups, n_narrow, place, ids, kept, rows)
    tile = min(256, rows)
    for base in range(0, rows, tile):
        sums[base : base + tile, :] = tile_sums(base, tile, grads, kept, width)


def row_kernel(groups, n_narrow, place, ids, table_in, accum, before, *refs):
    count = len(groups)
    grads, (new_table, new_accum), kept = refs[:count], refs[count : count + 2], refs[count + 2 : 2 * count + 2]
    table, fresh_out, done, spread, sems = refs[2 * count + 2 :]
    arrive = pltpu.make_async_copy(table_in, table, sems.at[0])
    arrive.start()
    rows, width = table.shape
    tile, lane = min(256, rows), 128
    bag_rows(groups, n_narrow, place, ids, kept, rows)
    leave = []
    for base in range(0, rows, tile):
        at = slice(base, base + tile)
        total = before[at, :] + tile_sums(base, tile, grads, kept, width)
        done[at, :] = total
        mean = jnp.sum(total * total, axis=1, keepdims=True) * (1.0 / width)
        spread[at, :] = jnp.broadcast_to(mean, (tile, lane))
    cuts = [slice(start, start + lane) for start in range(0, rows, lane)]
    fresh_out[...] = accum[...] + jnp.concatenate([spread[cut, :].T[:1, :] for cut in cuts], axis=1)

    def depart(source, target):
        move = pltpu.make_async_copy(source, target, sems.at[1 + len(leave)])
        move.start()
        leave.append(move)

    depart(fresh_out, new_accum)
    rate = 0.1 / (jnp.sqrt(fresh_out[...]) + 1e-8)
    arrive.wait()
    for cut in cuts:
        by_row = jnp.broadcast_to(rate[:, cut], (lane, lane)).T
        for h in range(width // lane):
            cols = slice(h * lane, (h + 1) * lane)
            table[cut, cols] = table[cut, cols] - done[cut, cols] * by_row
        depart(table.at[cut, :], new_table.at[cut, :])
    for move in leave:
        move.wait()


def early_part(groups, place, ids, grads, n_narrow, rows):
    samples, width = grads[0].shape[1:]
    vmem = pl.BlockSpec(memory_space=pltpu.VMEM)
    return pl.pallas_call(
        functools.partial(early_kernel, groups, n_narrow),
        out_shape=jax.ShapeDtypeStruct((rows, width), jnp.float32),
        in_specs=[pl.BlockSpec(memory_space=pltpu.SMEM), vmem] + [vmem] * len(grads),
        out_specs=vmem,
        scratch_shapes=[pltpu.VMEM((2, 16, len(pieces) * samples), jnp.int16) for pieces in groups],
        compiler_params=pltpu.CompilerParams(vmem_limit_bytes=14 * 2**20),
        cost_estimate=pl.CostEstimate(flops=0, bytes_accessed=0, transcendentals=0),
    )(place, ids, *grads)


def row_part(groups, place, ids, grads, n_narrow, table, accum, before):
    rows, width = table.shape
    samples = grads[0].shape[1]
    vmem, hbm = pl.BlockSpec(memory_space=pltpu.VMEM), pl.BlockSpec(memory_space=pltpu.HBM)
    return pl.pallas_call(
        functools.partial(row_kernel, groups, n_narrow),
        out_shape=(
            jax.ShapeDtypeStruct((rows, width), jnp.float32),
            jax.ShapeDtypeStruct((1, rows), jnp.float32),
        ),
        in_specs=[pl.BlockSpec(memory_space=pltpu.SMEM), vmem, hbm, vmem, vmem] + [vmem] * len(grads),
        out_specs=(hbm, hbm),
        scratch_shapes=[pltpu.VMEM((2, 16, len(pieces) * samples), jnp.int16) for pieces in groups]
        + [
            pltpu.VMEM((rows, width), jnp.float32),
            pltpu.VMEM((1, rows), jnp.float32),
            pltpu.VMEM((rows, width), jnp.float32),
            pltpu.VMEM((rows, 128), jnp.float32),
            pltpu.SemaphoreType.DMA((2 + rows // 128,)),
        ],
        compiler_params=pltpu.CompilerParams(vmem_limit_bytes=14 * 2**20),
        cost_estimate=pl.CostEstimate(
            flops=2 * rows * samples * width * sum(len(pieces) for pieces in groups),
            bytes_accessed=8 * rows * width,
            transcendentals=0,
        ),
    )(place, ids, table, accum, before, *grads)


def row_sums(grads, ids, offset, count):
    local = ids - offset
    local = jnp.where((local >= 0) & (local < count), local, count)
    result = jnp.zeros((count, grads.shape[1]), jnp.float32)
    for slot in range(ids.shape[1]):
        result = result + jax.ops.segment_sum(grads, local[:, slot], num_segments=count + 1)[:count]
    return result


def plain_body(dense, pooled, w_top, bias, d_hidden, bag_ids, tables, accum):
    samples = dense.shape[0]
    width = dense.shape[1]
    n_wide = lax.axis_size("wide")
    n_narrow = lax.axis_size("narrow")
    total = samples * n_wide * n_narrow
    feats = jnp.concatenate([dense[:, None, :], pooled], axis=1)
    count = feats.shape[1]
    low_i, low_j = np.tril_indices(count, -1)
    zmat = jnp.einsum("bfd,bgd->bfg", feats, feats, preferred_element_type=jnp.float32)
    z_in = jnp.concatenate([dense.astype(jnp.float32), zmat[:, low_i, low_j]], axis=1).astype(
        jnp.bfloat16
    )
    pre = jnp.dot(z_in, w_top.T, preferred_element_type=jnp.float32) + bias
    sig = jax.nn.sigmoid(pre)
    slope = sig * (1.0 + pre * (1.0 - sig))
    dpre = (d_hidden.astype(jnp.float32) * slope).astype(jnp.bfloat16)
    dz_full = jnp.dot(dpre, w_top, preferred_element_type=jnp.float32)
    dpairs = dz_full[:, width:]
    dmat = jnp.zeros((samples, count * count), jnp.float32).at[:, low_i * count + low_j].set(dpairs)
    dmat = dmat.reshape(samples, count, count)
    dsym = (dmat + jnp.transpose(dmat, (0, 2, 1))).astype(jnp.bfloat16)
    dfeat = jnp.einsum("bfg,bgd->bfd", dsym, feats, preferred_element_type=jnp.float32)
    dpooled = dfeat[:, 1:, :].astype(jnp.bfloat16)
    part = lax.slice_in_dim(dpre, 0, w_top.shape[0] // n_wide * lax.axis_size("wide"), axis=1)
    wide_part = lax.psum_scatter(
        jnp.dot(part.T, z_in, preferred_element_type=jnp.float32),
        "wide",
        scatter_dimension=0,
        tiled=True,
    )
    w_grad = lax.psum(wide_part, "narrow") / math.sqrt(total)
    owned = lax.all_to_all(dpooled, "wide", split_axis=1, concat_axis=0, tiled=True).reshape(
        n_wide * samples, width
    )
    bag = bag_ids.shape[2]
    ids_four = bag_ids[0].reshape(n_wide, n_narrow, samples, bag)
    rows_dev = tables.shape[1]
    narrow_pos = lax.axis_index("narrow")
    every = lax.all_gather(owned, "narrow", axis=0, tiled=True)
    ids_all = jnp.transpose(ids_four, (1, 0, 2, 3)).reshape(-1, bag)
    row_grad = row_sums(every.astype(jnp.float32), ids_all, narrow_pos * rows_dev, rows_dev)
    acc_new = accum[0] + jnp.mean(row_grad * row_grad, axis=1)
    table_new = tables[0] - 0.1 * row_grad / (jnp.sqrt(acc_new)[:, None] + 1e-08)
    return (table_new[None], acc_new[None], w_grad)


def body(dense, pooled, w_top, bias, d_hidden, bag_ids, tables, accum):
    n_wide, n_narrow = lax.axis_size("wide"), lax.axis_size("narrow")
    samples, count = dense.shape[0], pooled.shape[1]
    rows, width = tables.shape[1:]
    inputs = w_top.shape[1]
    total = samples * n_wide * n_narrow
    if n_narrow != 4 or n_wide & (n_wide - 1) or count != n_wide or total * width > 2**21:
        return plain_body(dense, pooled, w_top, bias, d_hidden, bag_ids, tables, accum)
    wide, narrow = lax.axis_index("wide"), lax.axis_index("narrow")
    core, chip = narrow % 2, narrow // 2
    place = jnp.stack([wide, core, narrow]).astype(jnp.int32)

    def swap(array, axis, bit):
        n = lax.axis_size(axis)
        return lax.ppermute(array, axis, [(i, i ^ bit) for i in range(n)])

    out = local_part(place, dense, pooled, w_top.T, bias, d_hidden)
    hold, give, keep, send = out
    ids = bag_ids[0].T
    tie = lambda *values: lax.optimization_barrier(values)
    taken = swap(give, "narrow", 1)
    received = swap(send, "narrow", 1)

    def reach(block, i):
        pairs = [
            (w * n_narrow + n, (w ^ (2 * i + (n + i) % 2)) * n_narrow + n) for w in range(n_wide) for n in range(n_narrow)
        ]
        return lax.ppermute(block, ("wide", "narrow"), pairs)

    got = {i: reach(jnp.stack([hold[i], taken[i]]), i) for i in (1, 0, 2, 3)}
    got[0], got[1], received = tie(got[0], got[1], received)
    half = keep + received
    columns = [reach(half[i].astype(jnp.bfloat16), i) for i in (0, 1, 2, 3)]
    near = jnp.concatenate([got[0], got[1]])
    across_near = swap(near, "narrow", 2)
    got[2], got[3], across_near = tie(got[2], got[3], across_near)
    across_far = [swap(got[2], "narrow", 2), swap(got[3], "narrow", 2)]
    mine = jnp.concatenate([near, got[2], got[3]])
    beside = swap(mine, "narrow", 1)
    pieces = lambda j, flip, those: tuple((j ^ s, i, flip) for i in those for s in range(2))
    half_way, every = range(n_wide // 4), range(n_wide // 2)
    sums = early_part([pieces(0, 0, every), pieces(2, 0, half_way)], place, ids, [mine, across_near], n_narrow, rows)
    *across_far, columns[0], columns[1], columns[2], columns[3], sums = tie(*across_far, *columns, sums)
    across = jnp.concatenate([across_near, *across_far])
    opposite = swap(across, "narrow", 1)
    part = sum(column.astype(jnp.float32) for column in columns) / math.sqrt(total)
    others = [swap(part.astype(jnp.bfloat16) if bit > 1 else part, "narrow", bit) for bit in (1, 2, 3)]
    late = jnp.concatenate(across_far)
    new_table, new_accum = row_part(
        [pieces(1, 1, every), pieces(2, 0, range(n_wide // 4, n_wide // 2)), pieces(3, 1, every)],
        place, ids, [beside, late, opposite], n_narrow, tables[0], accum, sums,
    )
    others[0], others[1], others[2], new_accum = tie(*others, new_accum)
    w_grad = sum((other.astype(jnp.float32) for other in others), part)[:inputs].T
    return (new_table[None], new_accum, w_grad)


def solution(mesh):
    placed = (
        P(("wide", "narrow"), None),
        P(("wide", "narrow"), None, None),
        P(),
        P(),
        P(("wide", "narrow"), None),
        P("wide", None, None),
        P("wide", "narrow", None),
        P("wide", "narrow"),
    )
    return jax.shard_map(
        body,
        mesh=mesh,
        in_specs=placed,
        out_specs=(P("wide", "narrow", None), P("wide", "narrow"), P("wide", None)),
        check_vma=False,
    )
```

```python
import functools
import math

import jax
import jax.numpy as jnp
import numpy as np
from jax import lax
from jax.experimental import pallas as pl
from jax.experimental.pallas import tpu as pltpu
from jax.sharding import PartitionSpec as P

NT = (((1,), (1,)), ((), ()))


def eye(n):
    r = lax.broadcasted_iota(jnp.int32, (n, n), 0)
    c = lax.broadcasted_iota(jnp.int32, (n, n), 1)
    return jnp.where(r == c, 1.0, 0.0).astype(jnp.bfloat16)


def local_kernel(place, dense_in, pooled_in, w_in, bias_in, d_hidden_in, *refs):
    dense, pooled, w_t, bias, d_hidden, pooled32, feat_t, zrows, z_t, dp_t, dpre_all, sems = refs[-12:]
    hold, give, keep, send = refs[:4]
    moves = [
        pltpu.make_async_copy(source, target, sems.at[i])
        for i, (source, target) in enumerate(
            ((pooled_in, pooled), (dense_in, dense), (w_in, w_t), (bias_in, bias), (d_hidden_in, d_hidden))
        )
    ]
    for move in moves:
        move.start()
    samples, width = dense.shape
    tables = pooled.shape[0] // samples
    count = tables + 1
    low_i, low_j = np.tril_indices(count, -1)
    pairs = len(low_i)
    of_pair = {}
    for p, (i, j) in enumerate(zip(low_i, low_j)):
        of_pair[int(i), int(j)] = of_pair[int(j), int(i)] = p
    wide, core = place[0], place[1]

    moves[0].wait()
    for h in range(width // 128):
        pooled32[h] = pooled[:, h * 128 : (h + 1) * 128].astype(jnp.float32)
    ident = eye(width)
    moves[1].wait()
    feat_t[0] = lax.dot_general(ident, dense[...], NT, preferred_element_type=jnp.float32)
    for t in range(tables):
        rows = jnp.concatenate(
            [pooled32[h, pl.ds(t, samples, stride=tables), :] for h in range(width // 128)], axis=1
        ).astype(jnp.bfloat16)
        feat_t[t + 1] = lax.dot_general(ident, rows, NT, preferred_element_type=jnp.float32)

    def products(c, sums):
        f = [feat_t[i, pl.ds(pl.multiple_of(c * 8, 8), 8), :] for i in range(count)]
        return tuple(s + f[i] * f[j] for s, i, j in zip(sums, low_i, low_j))

    zero = jnp.zeros((8, samples), jnp.float32)
    sums = lax.fori_loop(0, width // 8, products, (zero,) * pairs, unroll=True)
    zrows[...] = jnp.zeros_like(zrows)
    for p in range(pairs):
        zrows[p : p + 1, :] = jnp.sum(sums[p], axis=0, keepdims=True)

    z_t[:width, :] = feat_t[0].astype(jnp.bfloat16)
    extra = z_t.shape[0] - width
    z_t[width:, :] = zrows[:extra, :].astype(jnp.bfloat16)
    z_pairs = zrows[...].T[:, :pairs].astype(jnp.bfloat16)
    for move in moves[2:]:
        move.wait()
    w_pairs = w_t[width : width + pairs, :]
    pre = (
        jnp.dot(dense[...], w_t[:width, :], preferred_element_type=jnp.float32)
        + jnp.dot(z_pairs, w_pairs, preferred_element_type=jnp.float32)
        + bias[...]
    )
    sig = 1.0 / (1.0 + jnp.exp(-pre))
    slope = sig * (1.0 + pre * (1.0 - sig))
    dpre = (d_hidden[...].astype(jnp.float32) * slope).astype(jnp.bfloat16)
    dsym = lax.dot_general(w_pairs, dpre, NT, preferred_element_type=jnp.float32)
    dsym = dsym.astype(jnp.bfloat16).astype(jnp.float32)

    spread = [jnp.broadcast_to(dsym[p : p + 1, :], (8, samples)) for p in range(pairs)]

    def gradients(c, carry):
        for h in range(2):
            at = pl.ds(pl.multiple_of(c * 16 + h * 8, 8), 8)
            f = [feat_t[i, at, :] for i in range(count)]
            for t in range(tables):
                total = None
                for g in range(count):
                    if g != t + 1:
                        term = spread[of_pair[t + 1, g]] * f[g]
                        total = term if total is None else total + term
                dp_t[t, at, :] = total
        return carry

    lax.fori_loop(0, width // 16, gradients, 0, unroll=True)
    ident_s = eye(samples)
    for i in range(tables // 2):
        for target, side in ((give, 1 - core), (hold, core)):
            held = dp_t[jnp.bitwise_xor(wide, 2 * i + jnp.bitwise_xor(side, i % 2))].astype(jnp.bfloat16)
            got = lax.dot_general(ident_s, held, NT, preferred_element_type=jnp.float32)
            target[i] = got.astype(jnp.bfloat16)
    block = keep.shape[2]
    dpre_all[...] = dpre
    for i in range(tables // 2):
        for target, side in ((send, 1 - core), (keep, core)):
            column = jnp.bitwise_xor(wide, 2 * i + jnp.bitwise_xor(side, i % 2)) * block
            mine = dpre_all[:, pl.ds(pl.multiple_of(column, block), block)]
            target[i] = jnp.dot(z_t[...], mine, preferred_element_type=jnp.float32)


def local_part(place, dense, pooled, w_t, bias, d_hidden):
    samples, width = dense.shape
    tables = pooled.shape[1]
    hidden = w_t.shape[1]
    padded = -(-w_t.shape[0] // 16) * 16
    vmem, hbm = pl.BlockSpec(memory_space=pltpu.VMEM), pl.BlockSpec(memory_space=pltpu.HBM)
    gradients = [(tables // 2, samples, width)] * 2
    operands = (dense, pooled.reshape(samples * tables, width), w_t, bias.reshape(1, hidden), d_hidden)
    return pl.pallas_call(
        local_kernel,
        out_shape=[jax.ShapeDtypeStruct(shape, jnp.bfloat16) for shape in gradients]
        + [jax.ShapeDtypeStruct((tables // 2, padded, hidden // tables), jnp.float32)] * 2,
        in_specs=[pl.BlockSpec(memory_space=pltpu.SMEM)] + [hbm] * 5,
        out_specs=[vmem] * (len(gradients) + 2),
        scratch_shapes=[
            pltpu.VMEM((samples, width), dense.dtype),
            pltpu.VMEM((samples * tables, width), pooled.dtype),
            pltpu.VMEM(w_t.shape, w_t.dtype),
            pltpu.VMEM((1, hidden), bias.dtype),
            pltpu.VMEM((samples, hidden), d_hidden.dtype),
            pltpu.VMEM((width // 128, samples * tables, 128), jnp.float32),
            pltpu.VMEM((tables + 1, width, samples), jnp.float32),
            pltpu.VMEM((128, samples), jnp.float32),
            pltpu.VMEM((padded, samples), jnp.bfloat16),
            pltpu.VMEM((tables, width, samples), jnp.float32),
            pltpu.VMEM((samples, hidden), jnp.bfloat16),
            pltpu.SemaphoreType.DMA((5,)),
        ],
        compiler_params=pltpu.CompilerParams(vmem_limit_bytes=14 * 2**20),
    )(place, *[pltpu.with_memory_space_constraint(x, pltpu.HBM) for x in operands])


def bag_rows(groups, n_narrow, place, ids, kept, rows):
    wide, core, narrow = place[0], place[1], place[2]
    step = kept[0].shape[1]
    samples = kept[0].shape[2] // len(groups[0])
    down = lax.broadcasted_iota(jnp.int32, (step, samples), 0)
    for pieces, keep in zip(groups, kept):
        for i, (j, k, flip) in enumerate(pieces):
            source = jnp.bitwise_xor(wide, 2 * k + jnp.bitwise_xor(core, (flip + k) % 2))
            at = source * n_narrow + jnp.bitwise_xor(narrow, j)
            local = ids[:, pl.ds(pl.multiple_of(at * samples, samples), samples)] - narrow * rows
            for s in range(2):
                keep[s, :, i * samples : (i + 1) * samples] = (
                    jnp.broadcast_to(local[s : s + 1, :], (step, samples)) - down
                ).astype(jnp.int16)


def tile_sums(base, tile, grads, kept, width):
    one, none = jnp.bfloat16(1), jnp.bfloat16(0)
    step = kept[0].shape[1]
    total = None
    for grad, keep in zip(grads, kept):
        a, b = keep[0], keep[1]
        parts = []
        for i in range(tile // step):
            want = jnp.int16(base + i * step)
            parts.append(jnp.where(a == want, one, none) + jnp.where(b == want, one, none))
        hot = jnp.concatenate(parts, axis=0)
        term = jnp.dot(hot, grad[...].reshape(-1, width), preferred_element_type=jnp.float32)
        total = term if total is None else total + term
    return total


def early_kernel(groups, n_narrow, place, ids, *refs):
    count = len(groups)
    grads, sums, kept = refs[:count], refs[count], refs[count + 1 :]
    rows, width = sums.shape
    bag_rows(groups, n_narrow, place, ids, kept, rows)
    tile = min(256, rows)
    for base in range(0, rows, tile):
        sums[base : base + tile, :] = tile_sums(base, tile, grads, kept, width)


def row_kernel(groups, n_narrow, place, ids, table_in, accum, before, *refs):
    count = len(groups)
    grads, (new_table, new_accum), kept = refs[:count], refs[count : count + 2], refs[count + 2 : 2 * count + 2]
    table, fresh_out, done, spread, sems = refs[2 * count + 2 :]
    arrive = pltpu.make_async_copy(table_in, table, sems.at[0])
    arrive.start()
    rows, width = table.shape
    tile, lane = min(256, rows), 128
    bag_rows(groups, n_narrow, place, ids, kept, rows)
    leave = []
    for base in range(0, rows, tile):
        at = slice(base, base + tile)
        total = before[at, :] + tile_sums(base, tile, grads, kept, width)
        done[at, :] = total
        mean = jnp.sum(total * total, axis=1, keepdims=True) * (1.0 / width)
        spread[at, :] = jnp.broadcast_to(mean, (tile, lane))
    cuts = [slice(start, start + lane) for start in range(0, rows, lane)]
    fresh_out[...] = accum[...] + jnp.concatenate([spread[cut, :].T[:1, :] for cut in cuts], axis=1)

    def depart(source, target):
        move = pltpu.make_async_copy(source, target, sems.at[1 + len(leave)])
        move.start()
        leave.append(move)

    depart(fresh_out, new_accum)
    rate = 0.1 / (jnp.sqrt(fresh_out[...]) + 1e-8)
    arrive.wait()
    for cut in cuts:
        by_row = jnp.broadcast_to(rate[:, cut], (lane, lane)).T
        for h in range(width // lane):
            cols = slice(h * lane, (h + 1) * lane)
            table[cut, cols] = table[cut, cols] - done[cut, cols] * by_row
        depart(table.at[cut, :], new_table.at[cut, :])
    for move in leave:
        move.wait()


def early_part(groups, place, ids, grads, n_narrow, rows):
    samples, width = grads[0].shape[1:]
    vmem = pl.BlockSpec(memory_space=pltpu.VMEM)
    return pl.pallas_call(
        functools.partial(early_kernel, groups, n_narrow),
        out_shape=jax.ShapeDtypeStruct((rows, width), jnp.float32),
        in_specs=[pl.BlockSpec(memory_space=pltpu.SMEM), vmem] + [vmem] * len(grads),
        out_specs=vmem,
        scratch_shapes=[pltpu.VMEM((2, 16, len(pieces) * samples), jnp.int16) for pieces in groups],
        compiler_params=pltpu.CompilerParams(vmem_limit_bytes=14 * 2**20),
        cost_estimate=pl.CostEstimate(flops=0, bytes_accessed=0, transcendentals=0),
    )(place, ids, *grads)


def row_part(groups, place, ids, grads, n_narrow, table, accum, before):
    rows, width = table.shape
    samples = grads[0].shape[1]
    vmem, hbm = pl.BlockSpec(memory_space=pltpu.VMEM), pl.BlockSpec(memory_space=pltpu.HBM)
    return pl.pallas_call(
        functools.partial(row_kernel, groups, n_narrow),
        out_shape=(
            jax.ShapeDtypeStruct((rows, width), jnp.float32),
            jax.ShapeDtypeStruct((1, rows), jnp.float32),
        ),
        in_specs=[pl.BlockSpec(memory_space=pltpu.SMEM), vmem, hbm, vmem, vmem] + [vmem] * len(grads),
        out_specs=(hbm, hbm),
        scratch_shapes=[pltpu.VMEM((2, 16, len(pieces) * samples), jnp.int16) for pieces in groups]
        + [
            pltpu.VMEM((rows, width), jnp.float32),
            pltpu.VMEM((1, rows), jnp.float32),
            pltpu.VMEM((rows, width), jnp.float32),
            pltpu.VMEM((rows, 128), jnp.float32),
            pltpu.SemaphoreType.DMA((2 + rows // 128,)),
        ],
        compiler_params=pltpu.CompilerParams(vmem_limit_bytes=14 * 2**20),
        cost_estimate=pl.CostEstimate(
            flops=2 * rows * samples * width * sum(len(pieces) for pieces in groups),
            bytes_accessed=8 * rows * width,
            transcendentals=0,
        ),
    )(place, ids, table, accum, before, *grads)


def row_sums(grads, ids, offset, count):
    local = ids - offset
    local = jnp.where((local >= 0) & (local < count), local, count)
    result = jnp.zeros((count, grads.shape[1]), jnp.float32)
    for slot in range(ids.shape[1]):
        result = result + jax.ops.segment_sum(grads, local[:, slot], num_segments=count + 1)[:count]
    return result


def plain_body(dense, pooled, w_top, bias, d_hidden, bag_ids, tables, accum):
    samples = dense.shape[0]
    width = dense.shape[1]
    n_wide = lax.axis_size("wide")
    n_narrow = lax.axis_size("narrow")
    total = samples * n_wide * n_narrow
    feats = jnp.concatenate([dense[:, None, :], pooled], axis=1)
    count = feats.shape[1]
    low_i, low_j = np.tril_indices(count, -1)
    zmat = jnp.einsum("bfd,bgd->bfg", feats, feats, preferred_element_type=jnp.float32)
    z_in = jnp.concatenate([dense.astype(jnp.float32), zmat[:, low_i, low_j]], axis=1).astype(
        jnp.bfloat16
    )
    pre = jnp.dot(z_in, w_top.T, preferred_element_type=jnp.float32) + bias
    sig = jax.nn.sigmoid(pre)
    slope = sig * (1.0 + pre * (1.0 - sig))
    dpre = (d_hidden.astype(jnp.float32) * slope).astype(jnp.bfloat16)
    dz_full = jnp.dot(dpre, w_top, preferred_element_type=jnp.float32)
    dpairs = dz_full[:, width:]
    dmat = jnp.zeros((samples, count * count), jnp.float32).at[:, low_i * count + low_j].set(dpairs)
    dmat = dmat.reshape(samples, count, count)
    dsym = (dmat + jnp.transpose(dmat, (0, 2, 1))).astype(jnp.bfloat16)
    dfeat = jnp.einsum("bfg,bgd->bfd", dsym, feats, preferred_element_type=jnp.float32)
    dpooled = dfeat[:, 1:, :].astype(jnp.bfloat16)
    part = lax.slice_in_dim(dpre, 0, w_top.shape[0] // n_wide * lax.axis_size("wide"), axis=1)
    wide_part = lax.psum_scatter(
        jnp.dot(part.T, z_in, preferred_element_type=jnp.float32),
        "wide",
        scatter_dimension=0,
        tiled=True,
    )
    w_grad = lax.psum(wide_part, "narrow") / math.sqrt(total)
    owned = lax.all_to_all(dpooled, "wide", split_axis=1, concat_axis=0, tiled=True).reshape(
        n_wide * samples, width
    )
    bag = bag_ids.shape[2]
    ids_four = bag_ids[0].reshape(n_wide, n_narrow, samples, bag)
    rows_dev = tables.shape[1]
    narrow_pos = lax.axis_index("narrow")
    every = lax.all_gather(owned, "narrow", axis=0, tiled=True)
    ids_all = jnp.transpose(ids_four, (1, 0, 2, 3)).reshape(-1, bag)
    row_grad = row_sums(every.astype(jnp.float32), ids_all, narrow_pos * rows_dev, rows_dev)
    acc_new = accum[0] + jnp.mean(row_grad * row_grad, axis=1)
    table_new = tables[0] - 0.1 * row_grad / (jnp.sqrt(acc_new)[:, None] + 1e-08)
    return (table_new[None], acc_new[None], w_grad)


def body(dense, pooled, w_top, bias, d_hidden, bag_ids, tables, accum):
    n_wide, n_narrow = lax.axis_size("wide"), lax.axis_size("narrow")
    samples, count = dense.shape[0], pooled.shape[1]
    rows, width = tables.shape[1:]
    inputs = w_top.shape[1]
    total = samples * n_wide * n_narrow
    fits = (n_wide, n_narrow, count, bag_ids.shape[2], samples) == (8, 4, 8, 2, 128) and inputs - width <= 48
    fits = fits and width % 128 == 0 and width <= 256 and rows % 256 == 0 and rows * n_narrow < 2**15
    fits = fits and w_top.shape[0] % (128 * n_wide) == 0 and w_top.shape[0] <= 2048
    if not fits:
        return plain_body(dense, pooled, w_top, bias, d_hidden, bag_ids, tables, accum)
    wide, narrow = lax.axis_index("wide"), lax.axis_index("narrow")
    core, chip = narrow % 2, narrow // 2
    place = jnp.stack([wide, core, narrow]).astype(jnp.int32)

    def swap(array, axis, bit):
        n = lax.axis_size(axis)
        return lax.ppermute(array, axis, [(i, i ^ bit) for i in range(n)])

    out = local_part(place, dense, pooled, w_top.T, bias, d_hidden)
    hold, give, keep, send = out
    ids = bag_ids[0].T
    tie = lambda *values: lax.optimization_barrier(values)
    taken = swap(give, "narrow", 1)
    received = swap(send, "narrow", 1)

    def reach(block, i):
        pairs = [
            (w * n_narrow + n, (w ^ (2 * i + (n + i) % 2)) * n_narrow + n) for w in range(n_wide) for n in range(n_narrow)
        ]
        return lax.ppermute(block, ("wide", "narrow"), pairs)

    got = {i: reach(jnp.stack([hold[i], taken[i]]), i) for i in (1, 0, 2, 3)}
    got[1], got[0], received = tie(got[1], got[0], received)
    half = keep + received
    columns = [reach(half[i].astype(jnp.bfloat16), i) for i in (0, 1, 2, 3)]
    near = jnp.concatenate([got[0], got[1]])
    across_near = swap(near, "narrow", 2)
    got[2], got[3], across_near = tie(got[2], got[3], across_near)
    across_far = [swap(got[2], "narrow", 2), swap(got[3], "narrow", 2)]
    mine = jnp.concatenate([near, got[2], got[3]])
    beside = swap(mine, "narrow", 1)
    pieces = lambda j, flip, those: tuple((j ^ s, i, flip) for i in those for s in range(2))
    half_way, every = range(n_wide // 4), range(n_wide // 2)
    sums = early_part([pieces(0, 0, every), pieces(2, 0, half_way)], place, ids, [mine, across_near], n_narrow, rows)
    *across_far, columns[0], columns[1], columns[2], columns[3], sums = tie(*across_far, *columns, sums)
    across = jnp.concatenate([across_near, *across_far])
    opposite = swap(across, "narrow", 1)
    part = sum(column.astype(jnp.float32) for column in columns) / math.sqrt(total)
    others = [swap(part.astype(jnp.bfloat16) if bit > 1 else part, "narrow", bit) for bit in (1, 2, 3)]
    late = jnp.concatenate(across_far)
    new_table, new_accum = row_part(
        [pieces(1, 1, every), pieces(2, 0, range(n_wide // 4, n_wide // 2)), pieces(3, 1, every)],
        place, ids, [beside, late, opposite], n_narrow, tables[0], accum, sums,
    )
    others[0], others[1], others[2], new_accum = tie(*others, new_accum)
    parts = [lax.reduce_precision(x, 8, 7) for x in (part, others[0])] + [x.astype(jnp.float32) for x in others[1:]]
    w_grad = ((parts[0] + parts[1]) + (parts[2] + parts[3]))[:inputs].T
    return (new_table[None], new_accum, w_grad)


def solution(mesh):
    placed = (
        P(("wide", "narrow"), None),
        P(("wide", "narrow"), None, None),
        P(),
        P(),
        P(("wide", "narrow"), None),
        P("wide", None, None),
        P("wide", "narrow", None),
        P("wide", "narrow"),
    )
    return jax.shard_map(
        body,
        mesh=mesh,
        in_specs=placed,
        out_specs=(P("wide", "narrow", None), P("wide", "narrow"), P("wide", None)),
        check_vma=False,
    )
```

```python
import functools
import math

import jax
import jax.numpy as jnp
import numpy as np
from jax import lax
from jax.experimental import pallas as pl
from jax.experimental.pallas import tpu as pltpu
from jax.sharding import PartitionSpec as P

NT = (((1,), (1,)), ((), ()))


def eye(n):
    r = lax.broadcasted_iota(jnp.int32, (n, n), 0)
    c = lax.broadcasted_iota(jnp.int32, (n, n), 1)
    return jnp.where(r == c, 1.0, 0.0).astype(jnp.bfloat16)


def local_kernel(place, dense_in, pooled_in, w_in, bias_in, d_hidden_in, *refs):
    dense, pooled, w_t, bias, d_hidden, pooled32, feat_t, zrows, z_t, dp_t, dpre_all, sems = refs[-12:]
    hold, give, keep, send = refs[:4]
    moves = [
        pltpu.make_async_copy(source, target, sems.at[i])
        for i, (source, target) in enumerate(
            ((pooled_in, pooled), (dense_in, dense), (w_in, w_t), (bias_in, bias), (d_hidden_in, d_hidden))
        )
    ]
    for move in moves:
        move.start()
    samples, width = dense.shape
    tables = pooled.shape[0] // samples
    count = tables + 1
    low_i, low_j = np.tril_indices(count, -1)
    pairs = len(low_i)
    of_pair = {}
    for p, (i, j) in enumerate(zip(low_i, low_j)):
        of_pair[int(i), int(j)] = of_pair[int(j), int(i)] = p
    wide, core = place[0], place[1]

    moves[0].wait()
    for h in range(width // 128):
        pooled32[h] = pooled[:, h * 128 : (h + 1) * 128].astype(jnp.float32)
    ident = eye(width)
    moves[1].wait()
    feat_t[0] = lax.dot_general(ident, dense[...], NT, preferred_element_type=jnp.float32)
    for t in range(tables):
        rows = jnp.concatenate(
            [pooled32[h, pl.ds(t, samples, stride=tables), :] for h in range(width // 128)], axis=1
        ).astype(jnp.bfloat16)
        feat_t[t + 1] = lax.dot_general(ident, rows, NT, preferred_element_type=jnp.float32)

    def products(c, sums):
        f = [feat_t[i, pl.ds(pl.multiple_of(c * 8, 8), 8), :] for i in range(count)]
        return tuple(s + f[i] * f[j] for s, i, j in zip(sums, low_i, low_j))

    zero = jnp.zeros((8, samples), jnp.float32)
    sums = lax.fori_loop(0, width // 8, products, (zero,) * pairs, unroll=True)
    zrows[...] = jnp.zeros_like(zrows)
    for p in range(pairs):
        zrows[p : p + 1, :] = jnp.sum(sums[p], axis=0, keepdims=True)

    z_t[:width, :] = feat_t[0].astype(jnp.bfloat16)
    extra = z_t.shape[0] - width
    z_t[width:, :] = zrows[:extra, :].astype(jnp.bfloat16)
    z_pairs = zrows[...].T[:, :pairs].astype(jnp.bfloat16)
    for move in moves[2:]:
        move.wait()
    w_pairs = w_t[width : width + pairs, :]
    pre = (
        jnp.dot(dense[...], w_t[:width, :], preferred_element_type=jnp.float32)
        + jnp.dot(z_pairs, w_pairs, preferred_element_type=jnp.float32)
        + bias[...]
    )
    sig = 1.0 / (1.0 + jnp.exp(-pre))
    slope = sig * (1.0 + pre * (1.0 - sig))
    dpre = (d_hidden[...].astype(jnp.float32) * slope).astype(jnp.bfloat16)
    dsym = lax.dot_general(w_pairs, dpre, NT, preferred_element_type=jnp.float32)
    dsym = dsym.astype(jnp.bfloat16).astype(jnp.float32)

    spread = [jnp.broadcast_to(dsym[p : p + 1, :], (8, samples)) for p in range(pairs)]

    def gradients(c, carry):
        for h in range(2):
            at = pl.ds(pl.multiple_of(c * 16 + h * 8, 8), 8)
            f = [feat_t[i, at, :] for i in range(count)]
            for t in range(tables):
                total = None
                for g in range(count):
                    if g != t + 1:
                        term = spread[of_pair[t + 1, g]] * f[g]
                        total = term if total is None else total + term
                dp_t[t, at, :] = total
        return carry

    lax.fori_loop(0, width // 16, gradients, 0, unroll=True)
    ident_s = eye(samples)
    for i in range(tables // 2):
        for target, side in ((give, 1 - core), (hold, core)):
            held = dp_t[jnp.bitwise_xor(wide, 2 * i + jnp.bitwise_xor(side, i % 2))].astype(jnp.bfloat16)
            got = lax.dot_general(ident_s, held, NT, preferred_element_type=jnp.float32)
            target[i] = got.astype(jnp.bfloat16)
    block = keep.shape[2]
    dpre_all[...] = dpre
    for i in range(tables // 2):
        for target, side in ((send, 1 - core), (keep, core)):
            column = jnp.bitwise_xor(wide, 2 * i + jnp.bitwise_xor(side, i % 2)) * block
            mine = dpre_all[:, pl.ds(pl.multiple_of(column, block), block)]
            target[i] = jnp.dot(z_t[...], mine, preferred_element_type=jnp.float32)


def local_part(place, dense, pooled, w_t, bias, d_hidden):
    samples, width = dense.shape
    tables = pooled.shape[1]
    hidden = w_t.shape[1]
    padded = -(-w_t.shape[0] // 16) * 16
    vmem, hbm = pl.BlockSpec(memory_space=pltpu.VMEM), pl.BlockSpec(memory_space=pltpu.HBM)
    gradients = [(tables // 2, samples, width)] * 2
    operands = (dense, pooled.reshape(samples * tables, width), w_t, bias.reshape(1, hidden), d_hidden)
    return pl.pallas_call(
        local_kernel,
        out_shape=[jax.ShapeDtypeStruct(shape, jnp.bfloat16) for shape in gradients]
        + [jax.ShapeDtypeStruct((tables // 2, padded, hidden // tables), jnp.float32)] * 2,
        in_specs=[pl.BlockSpec(memory_space=pltpu.SMEM)] + [hbm] * 5,
        out_specs=[vmem] * (len(gradients) + 2),
        scratch_shapes=[
            pltpu.VMEM((samples, width), dense.dtype),
            pltpu.VMEM((samples * tables, width), pooled.dtype),
            pltpu.VMEM(w_t.shape, w_t.dtype),
            pltpu.VMEM((1, hidden), bias.dtype),
            pltpu.VMEM((samples, hidden), d_hidden.dtype),
            pltpu.VMEM((width // 128, samples * tables, 128), jnp.float32),
            pltpu.VMEM((tables + 1, width, samples), jnp.float32),
            pltpu.VMEM((128, samples), jnp.float32),
            pltpu.VMEM((padded, samples), jnp.bfloat16),
            pltpu.VMEM((tables, width, samples), jnp.float32),
            pltpu.VMEM((samples, hidden), jnp.bfloat16),
            pltpu.SemaphoreType.DMA((5,)),
        ],
        compiler_params=pltpu.CompilerParams(vmem_limit_bytes=14 * 2**20),
    )(place, *[pltpu.with_memory_space_constraint(x, pltpu.HBM) for x in operands])


def bag_rows(groups, n_narrow, place, ids, kept, rows):
    wide, core, narrow = place[0], place[1], place[2]
    step = kept[0].shape[1]
    samples = kept[0].shape[2] // len(groups[0])
    down = lax.broadcasted_iota(jnp.int32, (step, samples), 0)
    for pieces, keep in zip(groups, kept):
        for i, (j, k, flip) in enumerate(pieces):
            source = jnp.bitwise_xor(wide, 2 * k + jnp.bitwise_xor(core, (flip + k) % 2))
            at = source * n_narrow + jnp.bitwise_xor(narrow, j)
            local = ids[:, pl.ds(pl.multiple_of(at * samples, samples), samples)] - narrow * rows
            for s in range(2):
                keep[s, :, i * samples : (i + 1) * samples] = (
                    jnp.broadcast_to(local[s : s + 1, :], (step, samples)) - down
                ).astype(jnp.int16)


def tile_sums(base, tile, grads, kept, width):
    one, none = jnp.bfloat16(1), jnp.bfloat16(0)
    step = kept[0].shape[1]
    total = None
    for grad, keep in zip(grads, kept):
        a, b = keep[0], keep[1]
        parts = []
        for i in range(tile // step):
            want = jnp.int16(base + i * step)
            parts.append(jnp.where(a == want, one, none) + jnp.where(b == want, one, none))
        hot = jnp.concatenate(parts, axis=0)
        term = jnp.dot(hot, grad[...].reshape(-1, width), preferred_element_type=jnp.float32)
        total = term if total is None else total + term
    return total


def early_kernel(groups, n_narrow, place, ids, *refs):
    count = len(groups)
    grads, sums, kept = refs[:count], refs[count], refs[count + 1 :]
    rows, width = sums.shape
    bag_rows(groups, n_narrow, place, ids, kept, rows)
    tile = 512 if rows % 512 == 0 else 256
    for base in range(0, rows, tile):
        sums[base : base + tile, :] = tile_sums(base, tile, grads, kept, width)


def row_kernel(groups, n_narrow, place, ids, table_in, accum, before, *refs):
    count = len(groups)
    grads, (new_table, new_accum), kept = refs[:count], refs[count : count + 2], refs[count + 2 : 2 * count + 2]
    table, fresh_out, done, spread, sems = refs[2 * count + 2 :]
    arrive = pltpu.make_async_copy(table_in, table, sems.at[0])
    arrive.start()
    rows, width = table.shape
    tile, lane = min(256, rows), 128
    bag_rows(groups, n_narrow, place, ids, kept, rows)
    leave = []
    for base in range(0, rows, tile):
        at = slice(base, base + tile)
        total = before[at, :] + tile_sums(base, tile, grads, kept, width)
        done[at, :] = total
        mean = jnp.sum(total * total, axis=1, keepdims=True) * (1.0 / width)
        spread[at, :] = jnp.broadcast_to(mean, (tile, lane))
    cuts = [slice(start, start + lane) for start in range(0, rows, lane)]
    fresh_out[...] = accum[...] + jnp.concatenate([spread[cut, :].T[:1, :] for cut in cuts], axis=1)

    def depart(source, target):
        move = pltpu.make_async_copy(source, target, sems.at[1 + len(leave)])
        move.start()
        leave.append(move)

    depart(fresh_out, new_accum)
    rate = 0.1 / (jnp.sqrt(fresh_out[...]) + 1e-8)
    arrive.wait()
    for cut in cuts:
        by_row = jnp.broadcast_to(rate[:, cut], (lane, lane)).T
        for h in range(width // lane):
            cols = slice(h * lane, (h + 1) * lane)
            table[cut, cols] = table[cut, cols] - done[cut, cols] * by_row
        depart(table.at[cut, :], new_table.at[cut, :])
    for move in leave:
        move.wait()


def early_part(groups, place, ids, grads, n_narrow, rows):
    samples, width = grads[0].shape[1:]
    vmem = pl.BlockSpec(memory_space=pltpu.VMEM)
    return pl.pallas_call(
        functools.partial(early_kernel, groups, n_narrow),
        out_shape=jax.ShapeDtypeStruct((rows, width), jnp.float32),
        in_specs=[pl.BlockSpec(memory_space=pltpu.SMEM), vmem] + [vmem] * len(grads),
        out_specs=vmem,
        scratch_shapes=[pltpu.VMEM((2, 16, len(pieces) * samples), jnp.int16) for pieces in groups],
        compiler_params=pltpu.CompilerParams(vmem_limit_bytes=14 * 2**20),
        cost_estimate=pl.CostEstimate(flops=0, bytes_accessed=0, transcendentals=0),
    )(place, ids, *grads)


def row_part(groups, place, ids, grads, n_narrow, table, accum, before):
    rows, width = table.shape
    samples = grads[0].shape[1]
    vmem, hbm = pl.BlockSpec(memory_space=pltpu.VMEM), pl.BlockSpec(memory_space=pltpu.HBM)
    return pl.pallas_call(
        functools.partial(row_kernel, groups, n_narrow),
        out_shape=(
            jax.ShapeDtypeStruct((rows, width), jnp.float32),
            jax.ShapeDtypeStruct((1, rows), jnp.float32),
        ),
        in_specs=[pl.BlockSpec(memory_space=pltpu.SMEM), vmem, hbm, vmem, vmem] + [vmem] * len(grads),
        out_specs=(hbm, hbm),
        scratch_shapes=[pltpu.VMEM((2, 16, len(pieces) * samples), jnp.int16) for pieces in groups]
        + [
            pltpu.VMEM((rows, width), jnp.float32),
            pltpu.VMEM((1, rows), jnp.float32),
            pltpu.VMEM((rows, width), jnp.float32),
            pltpu.VMEM((rows, 128), jnp.float32),
            pltpu.SemaphoreType.DMA((2 + rows // 128,)),
        ],
        compiler_params=pltpu.CompilerParams(vmem_limit_bytes=14 * 2**20),
        cost_estimate=pl.CostEstimate(
            flops=2 * rows * samples * width * sum(len(pieces) for pieces in groups),
            bytes_accessed=8 * rows * width,
            transcendentals=0,
        ),
    )(place, ids, table, accum, before, *grads)


def row_sums(grads, ids, offset, count):
    local = ids - offset
    local = jnp.where((local >= 0) & (local < count), local, count)
    result = jnp.zeros((count, grads.shape[1]), jnp.float32)
    for slot in range(ids.shape[1]):
        result = result + jax.ops.segment_sum(grads, local[:, slot], num_segments=count + 1)[:count]
    return result


def plain_body(dense, pooled, w_top, bias, d_hidden, bag_ids, tables, accum):
    samples = dense.shape[0]
    width = dense.shape[1]
    n_wide = lax.axis_size("wide")
    n_narrow = lax.axis_size("narrow")
    total = samples * n_wide * n_narrow
    feats = jnp.concatenate([dense[:, None, :], pooled], axis=1)
    count = feats.shape[1]
    low_i, low_j = np.tril_indices(count, -1)
    zmat = jnp.einsum("bfd,bgd->bfg", feats, feats, preferred_element_type=jnp.float32)
    z_in = jnp.concatenate([dense.astype(jnp.float32), zmat[:, low_i, low_j]], axis=1).astype(
        jnp.bfloat16
    )
    pre = jnp.dot(z_in, w_top.T, preferred_element_type=jnp.float32) + bias
    sig = jax.nn.sigmoid(pre)
    slope = sig * (1.0 + pre * (1.0 - sig))
    dpre = (d_hidden.astype(jnp.float32) * slope).astype(jnp.bfloat16)
    dz_full = jnp.dot(dpre, w_top, preferred_element_type=jnp.float32)
    dpairs = dz_full[:, width:]
    dmat = jnp.zeros((samples, count * count), jnp.float32).at[:, low_i * count + low_j].set(dpairs)
    dmat = dmat.reshape(samples, count, count)
    dsym = (dmat + jnp.transpose(dmat, (0, 2, 1))).astype(jnp.bfloat16)
    dfeat = jnp.einsum("bfg,bgd->bfd", dsym, feats, preferred_element_type=jnp.float32)
    dpooled = dfeat[:, 1:, :].astype(jnp.bfloat16)
    part = lax.slice_in_dim(dpre, 0, w_top.shape[0] // n_wide * lax.axis_size("wide"), axis=1)
    wide_part = lax.psum_scatter(
        jnp.dot(part.T, z_in, preferred_element_type=jnp.float32),
        "wide",
        scatter_dimension=0,
        tiled=True,
    )
    w_grad = lax.psum(wide_part, "narrow") / math.sqrt(total)
    owned = lax.all_to_all(dpooled, "wide", split_axis=1, concat_axis=0, tiled=True).reshape(
        n_wide * samples, width
    )
    bag = bag_ids.shape[2]
    ids_four = bag_ids[0].reshape(n_wide, n_narrow, samples, bag)
    rows_dev = tables.shape[1]
    narrow_pos = lax.axis_index("narrow")
    every = lax.all_gather(owned, "narrow", axis=0, tiled=True)
    ids_all = jnp.transpose(ids_four, (1, 0, 2, 3)).reshape(-1, bag)
    row_grad = row_sums(every.astype(jnp.float32), ids_all, narrow_pos * rows_dev, rows_dev)
    acc_new = accum[0] + jnp.mean(row_grad * row_grad, axis=1)
    table_new = tables[0] - 0.1 * row_grad / (jnp.sqrt(acc_new)[:, None] + 1e-08)
    return (table_new[None], acc_new[None], w_grad)


def body(dense, pooled, w_top, bias, d_hidden, bag_ids, tables, accum):
    n_wide, n_narrow = lax.axis_size("wide"), lax.axis_size("narrow")
    samples, count = dense.shape[0], pooled.shape[1]
    rows, width = tables.shape[1:]
    inputs = w_top.shape[1]
    total = samples * n_wide * n_narrow
    fits = (n_wide, n_narrow, count, bag_ids.shape[2], samples) == (8, 4, 8, 2, 128) and inputs - width <= 48
    fits = fits and width % 128 == 0 and width <= 256 and rows % 256 == 0 and rows * n_narrow < 2**15
    fits = fits and w_top.shape[0] % (128 * n_wide) == 0 and w_top.shape[0] <= 2048
    if not fits:
        return plain_body(dense, pooled, w_top, bias, d_hidden, bag_ids, tables, accum)
    wide, narrow = lax.axis_index("wide"), lax.axis_index("narrow")
    core, chip = narrow % 2, narrow // 2
    place = jnp.stack([wide, core, narrow]).astype(jnp.int32)

    def swap(array, axis, bit):
        n = lax.axis_size(axis)
        return lax.ppermute(array, axis, [(i, i ^ bit) for i in range(n)])

    out = local_part(place, dense, pooled, w_top.T, bias, d_hidden)
    hold, give, keep, send = out
    ids = bag_ids[0].T
    tie = lambda *values: lax.optimization_barrier(values)
    taken = swap(give, "narrow", 1)
    received = swap(send, "narrow", 1)

    def reach(block, i):
        pairs = [
            (w * n_narrow + n, (w ^ (2 * i + (n + i) % 2)) * n_narrow + n) for w in range(n_wide) for n in range(n_narrow)
        ]
        return lax.ppermute(block, ("wide", "narrow"), pairs)

    got = {i: reach(jnp.stack([hold[i], taken[i]]), i) for i in (1, 0, 2, 3)}
    got[1], got[0], received = tie(got[1], got[0], received)
    half = keep + received
    columns = [reach(half[i].astype(jnp.bfloat16), i) for i in (0, 1, 2, 3)]
    near = jnp.concatenate([got[0], got[1]])
    across_near = swap(near, "narrow", 2)
    got[2], got[3], across_near = tie(got[2], got[3], across_near)
    across_far = [swap(got[2], "narrow", 2), swap(got[3], "narrow", 2)]
    mine = jnp.concatenate([near, got[2], got[3]])
    beside = swap(mine, "narrow", 1)
    pieces = lambda j, flip, those: tuple((j ^ s, i, flip) for i in those for s in range(2))
    half_way, every = range(n_wide // 4), range(n_wide // 2)
    sums = early_part([pieces(0, 0, every), pieces(2, 0, half_way)], place, ids, [mine, across_near], n_narrow, rows)
    *across_far, columns[0], columns[1], columns[2], columns[3], sums = tie(*across_far, *columns, sums)
    across = jnp.concatenate([across_near, *across_far])
    opposite = swap(across, "narrow", 1)
    part = sum(column.astype(jnp.float32) for column in columns) / math.sqrt(total)
    others = [swap(part.astype(jnp.bfloat16) if bit > 1 else part, "narrow", bit) for bit in (1, 2, 3)]
    late = jnp.concatenate(across_far)
    new_table, new_accum = row_part(
        [pieces(1, 1, every), pieces(2, 0, range(n_wide // 4, n_wide // 2)), pieces(3, 1, every)],
        place, ids, [beside, late, opposite], n_narrow, tables[0], accum, sums,
    )
    others[0], others[1], others[2], new_accum = tie(*others, new_accum)
    parts = [lax.reduce_precision(x, 8, 7) for x in (part, others[0])] + [x.astype(jnp.float32) for x in others[1:]]
    w_grad = ((parts[0] + parts[1]) + (parts[2] + parts[3]))[:inputs].T
    return (new_table[None], new_accum, w_grad)


def solution(mesh):
    placed = (
        P(("wide", "narrow"), None),
        P(("wide", "narrow"), None, None),
        P(),
        P(),
        P(("wide", "narrow"), None),
        P("wide", None, None),
        P("wide", "narrow", None),
        P("wide", "narrow"),
    )
    return jax.shard_map(
        body,
        mesh=mesh,
        in_specs=placed,
        out_specs=(P("wide", "narrow", None), P("wide", "narrow"), P("wide", None)),
        check_vma=False,
    )
```
